256 devices in a mesh: row: 4 (over x), col: 4 (over y), dp: 16 (over z, core).
Axes of the slice: x: 4, y: 4, z: 8, core: 2. Of those that a mesh axis runs over, the one named last changes fastest.
Arguments:
- tokens_in: bfloat16 [3072, 4096], P(('col', 'dp'), 'row'), may hold values from -6 to 6
- out_grad: bfloat16 [3072, 4096], P(('col', 'dp'), 'row'), may hold values from -1.5 to 1.5
- gate_weight: bfloat16 [4096, 14336], P('row', 'col'), may hold values from -0.125 to 0.125
- up_weight: bfloat16 [4096, 14336], P('row', 'col'), may hold values from -0.125 to 0.125
- down_weight: bfloat16 [14336, 4096], P('col', 'row'), may hold values from -0.0625 to 0.0625
- inner_mask: int32 [32, 112], P('row', 'col'), may hold values from 0 to 1, as said below
- outer_mask: int32 [112, 32], P('col', 'row'), may hold values from 0 to 1, as said below
Outputs:
- layer_out: bfloat16 [3072, 4096], P(('col', 'dp'), 'row')
- input_grad: bfloat16 [3072, 4096], P(('col', 'dp'), 'row')
- gate_grad: bfloat16 [4096, 14336], P('row', ('col', 'dp'))
- up_grad: bfloat16 [4096, 14336], P('row', ('col', 'dp'))
- down_grad: bfloat16 [14336, 4096], P(('col', 'dp'), 'row')
The draws below stay inside these ranges and needn't reach their ends.
Inputs may be any that keep to these rules, and one draw needn't show every extreme that they name: `inner_mask`: 1 keeps a 128 x 128 block of the gate and up projections, 0 drops it; the share of kept blocks differs from one device's tile to another, and a device's tile may keep all of its blocks. `outer_mask`: 1 keeps a 128 x 128 block of the down projection, 0 drops it; the share of kept blocks differs from one device's tile to another, and a device's tile may keep all of its blocks.
All inputs are finite; a program needn't handle non-finite values.
Results may differ from the reference program's by a relative error of at most 0.035.
Values may be sent and summed in bfloat16 or wider, within the bound.
A program may use at most 192 MiB of HBM per device.

```python
import jax
import jax.numpy as jnp
from jax import lax

D = 4096
FF = 14336
BLOCK = 128
TOKENS = 3072
N_ROW = 4
N_COL = 4
N_DP = 16


def tiled_mask(key, grid_rows, grid_cols, tile_rows, tile_cols):
    level_key, full_key, block_key = jax.random.split(key, 3)
    tiles = grid_rows * grid_cols
    levels = jax.random.randint(level_key, (tiles,), 1, 8)
    chosen = jax.random.randint(full_key, (), 0, tiles)
    levels = jnp.where(jnp.arange(tiles) == chosen, 8, levels).reshape(grid_rows, grid_cols)
    spread = jnp.repeat(jnp.repeat(levels, tile_rows, axis=0), tile_cols, axis=1)
    picks = jax.random.randint(block_key, (grid_rows * tile_rows, grid_cols * tile_cols), 0, 8)
    return (picks < spread).astype(jnp.int32)


def draw_inner_mask(key, part):
    key = jax.random.fold_in(key, 11)
    return tiled_mask(key, N_ROW, N_COL, D // BLOCK // N_ROW, FF // BLOCK // N_COL)


def draw_outer_mask(key, part):
    key = jax.random.fold_in(key, 12)
    return tiled_mask(key, N_COL, N_ROW, FF // BLOCK // N_COL, D // BLOCK // N_ROW)


def steps_of(own_key, dims, shards, least, high):
    def one(dim, shards_of):
        heights = jax.random.uniform(jax.random.fold_in(jax.random.fold_in(own_key, 6), dim), (shards_of,), jnp.float32, least / len(shards), high / len(shards))
        return jnp.repeat(jnp.exp(heights), dims[dim] // shards_of).reshape((-1,) + (1,) * (len(dims) - dim - 1))

    factor_of = one(*shards[0])
    for cut in shards[1:]:
        factor_of = factor_of * one(*cut)
    return factor_of


def centred(own_key, shape, deviation, limit, pieces=(), dtype=jnp.bfloat16):
    drawn = jax.random.normal(own_key, shape, jnp.float32) * deviation
    if len(pieces) > 0:
        drawn = steps_of(own_key, shape, pieces, -0.22, 0.18) * drawn
    return jnp.clip(drawn, min=-limit, max=limit).astype(dtype)


def setup_inputs(seed: int = 0) -> dict:
    key_of = jax.random.split(jax.random.key(seed), 8)
    return {
        "tokens_in": centred(key_of[0], (TOKENS, D), 1.0, 6.0, ((0, 64), (1, 4))),
        "out_grad": centred(key_of[1], (TOKENS, D), 0.25, 1.5, ((0, 64), (1, 4))),
        "gate_weight": centred(key_of[2], (D, FF), (D // 2) ** -0.5, 0.125, ((0, 4), (1, 4))),
        "up_weight": centred(key_of[3], (D, FF), (D // 2) ** -0.5, 0.125, ((0, 4), (1, 4))),
        "down_weight": centred(key_of[4], (FF, D), (FF // 2) ** -0.5, 0.0625, ((0, 4), (1, 4))),
        "inner_mask": draw_inner_mask(jax.random.fold_in(key_of[7], 71), 0),
        "outer_mask": draw_outer_mask(jax.random.fold_in(key_of[7], 71), 0),
    }


def expand_blocks(blocked):
    widened = jnp.repeat(blocked.astype(jnp.bfloat16), BLOCK, axis=0)
    return jnp.repeat(widened, BLOCK, axis=1)


def rounded(values):
    return lax.optimization_barrier(values.astype(jnp.bfloat16)).astype(jnp.float32)


def split_product(left, right, parts):
    depth = left.shape[1] // parts
    left_parts = left.reshape(left.shape[0], parts, depth).transpose(1, 0, 2)
    right_parts = right.reshape(parts, depth, right.shape[1])

    def add_part(total, pair):
        return total + rounded(jnp.dot(pair[0], pair[1], preferred_element_type=jnp.float32)), None

    total, ignored = lax.scan(add_part, jnp.zeros((left.shape[0], right.shape[1]), jnp.float32), (left_parts, right_parts))
    return total


def replica_split(values):
    cols = values.shape[1]
    return values.reshape(N_COL, N_DP, -1, cols).transpose(1, 0, 2, 3).reshape(N_DP, -1, cols)


def replica_sum(left, right):
    def add_part(total, pair):
        return total + rounded(jnp.dot(pair[0].T, pair[1], preferred_element_type=jnp.float32)), None

    total, ignored = lax.scan(add_part, jnp.zeros((left.shape[1], right.shape[1]), jnp.float32), (replica_split(left), replica_split(right)))
    return total


def reference(tokens_in, out_grad, gate_weight, up_weight, down_weight, inner_mask, outer_mask):
    inner_full = expand_blocks(inner_mask)
    outer_full = expand_blocks(outer_mask)
    gate_eff = gate_weight * inner_full
    up_eff = up_weight * inner_full
    down_eff = down_weight * outer_full
    gate_vals = split_product(tokens_in, gate_eff, N_ROW)
    up_vals = split_product(tokens_in, up_eff, N_ROW)
    hidden = (jax.nn.silu(gate_vals) * up_vals).astype(jnp.bfloat16)
    layer_out = split_product(hidden, down_eff, N_COL).astype(jnp.bfloat16)
    hidden_grad = split_product(out_grad, down_eff.T, N_ROW)
    sig = jax.nn.sigmoid(gate_vals)
    gate_back = (hidden_grad * up_vals * sig * (1.0 + gate_vals * (1.0 - sig))).astype(jnp.bfloat16)
    up_back = (hidden_grad * gate_vals * sig).astype(jnp.bfloat16)
    count = tokens_in.shape[0]
    width = tokens_in.shape[1]
    left_joined = jnp.concatenate([gate_back.reshape(count, N_COL, -1), up_back.reshape(count, N_COL, -1)], axis=2).reshape(count, -1)
    right_joined = jnp.concatenate([gate_eff.T.reshape(N_COL, -1, width), up_eff.T.reshape(N_COL, -1, width)], axis=1).reshape(-1, width)
    input_grad = split_product(left_joined, right_joined, N_COL).astype(jnp.bfloat16)
    gate_grad = (replica_sum(tokens_in, gate_back) * inner_full.astype(jnp.float32)).astype(jnp.bfloat16)
    up_grad = (replica_sum(tokens_in, up_back) * inner_full.astype(jnp.float32)).astype(jnp.bfloat16)
    down_grad = (replica_sum(hidden, out_grad) * outer_full.astype(jnp.float32)).astype(jnp.bfloat16)
    return (layer_out, input_grad, gate_grad, up_grad, down_grad)
```

```python
import jax
import jax.numpy as jnp
from jax import lax
from jax.sharding import PartitionSpec as P


def expand_blocks(blocked, edge):
    count_rows, count_cols = blocked.shape
    scaled = blocked.astype(jnp.bfloat16)
    widened = jnp.broadcast_to(scaled[:, None, :, None], (count_rows, edge, count_cols, edge))
    return widened.reshape(count_rows * edge, count_cols * edge)


def contract_last(left, right):
    return lax.dot_general(
        left, right, (((1,), (1,)), ((), ())), preferred_element_type=jnp.float32
    )


def contract_first(left, right):
    return lax.dot_general(
        left, right, (((0,), (0,)), ((), ())), preferred_element_type=jnp.float32
    )


def gated_grads(gate_vals, up_vals, hidden_grad):
    sig = jax.nn.sigmoid(gate_vals)
    gate_back = (hidden_grad * up_vals * sig * (1.0 + gate_vals * (1.0 - sig))).astype(jnp.bfloat16)
    up_back = (hidden_grad * gate_vals * sig).astype(jnp.bfloat16)
    return (gate_back, up_back)


def scatter_tokens(part):
    over_col = lax.psum_scatter(
        part.astype(jnp.bfloat16), "col", scatter_dimension=0, tiled=True
    )
    return lax.psum_scatter(over_col, "dp", scatter_dimension=0, tiled=True)


def on_device(tokens_in, out_grad, gate_weight, up_weight, down_weight, inner_mask, outer_mask):
    edge = gate_weight.shape[0] // inner_mask.shape[0]
    piece = gate_weight.shape[1] // lax.axis_size("dp")
    offset = lax.axis_index("dp") * piece
    inner_slice = lax.dynamic_slice_in_dim(expand_blocks(inner_mask, edge), offset, piece, 1)
    outer_slice = lax.dynamic_slice_in_dim(expand_blocks(outer_mask, edge), offset, piece, 0)
    gate_eff = lax.dynamic_slice_in_dim(gate_weight, offset, piece, 1) * inner_slice
    up_eff = lax.dynamic_slice_in_dim(up_weight, offset, piece, 1) * inner_slice
    down_eff = lax.dynamic_slice_in_dim(down_weight, offset, piece, 0) * outer_slice
    joined = jnp.concatenate([gate_eff, up_eff], axis=1)
    inputs_all = lax.all_gather(tokens_in, ("col", "dp"), axis=0, tiled=True)
    grads_all = lax.all_gather(out_grad, ("col", "dp"), axis=0, tiled=True)
    parts = jnp.concatenate(
        [
            jnp.dot(inputs_all, joined, preferred_element_type=jnp.float32),
            contract_last(grads_all, down_eff),
        ],
        axis=1,
    ).astype(jnp.bfloat16)
    summed = lax.psum_scatter(parts, "row", scatter_dimension=0, tiled=True).astype(jnp.float32)
    gate_vals = summed[:, :piece]
    up_vals = summed[:, piece : 2 * piece]
    hidden_grad = summed[:, 2 * piece :]
    hidden_share = (jax.nn.silu(gate_vals) * up_vals).astype(jnp.bfloat16)
    gate_share, up_share = gated_grads(gate_vals, up_vals, hidden_grad)
    shares = jnp.concatenate([gate_share, up_share, hidden_share], axis=1)
    whole = lax.all_gather(shares, "row", axis=0, tiled=True)
    backs = whole[:, : 2 * piece]
    hidden = whole[:, 2 * piece :]
    layer_out = scatter_tokens(jnp.dot(hidden, down_eff, preferred_element_type=jnp.float32))
    input_grad = scatter_tokens(contract_last(backs, joined))
    back_grads = contract_first(inputs_all, backs)
    inner_scale = inner_slice.astype(jnp.float32)
    gate_grad = (back_grads[:, :piece] * inner_scale).astype(jnp.bfloat16)
    up_grad = (back_grads[:, piece:] * inner_scale).astype(jnp.bfloat16)
    down_grad = (contract_first(hidden, grads_all) * outer_slice.astype(jnp.float32)).astype(
        jnp.bfloat16
    )
    return (layer_out, input_grad, gate_grad, up_grad, down_grad)


def solution(mesh):
    placed = (
        P(("col", "dp"), "row"),
        P(("col", "dp"), "row"),
        P("row", "col"),
        P("row", "col"),
        P("col", "row"),
        P("row", "col"),
        P("col", "row"),
    )
    return jax.shard_map(
        on_device,
        mesh=mesh,
        in_specs=placed,
        out_specs=(
            P(("col", "dp"), "row"),
            P(("col", "dp"), "row"),
            P("row", ("col", "dp")),
            P("row", ("col", "dp")),
            P(("col", "dp"), "row"),
        ),
        check_vma=False,
    )
```

```python
import jax
import jax.numpy as jnp
from jax import lax
from jax.experimental import pallas as pl
from jax.experimental.pallas import tpu as pltpu
from jax.sharding import PartitionSpec as P

MESH = pl.DeviceIdType.MESH
F32 = jnp.float32
BF16 = jnp.bfloat16
CHUNKS = 3
ROWS = 16
SLOTS = 8
GROUPS = ((0, 1), (1, 3), (3, 5), (5, 8))


def expand_blocks(blocked, edge):
    count_rows, count_cols = blocked.shape
    scaled = blocked.astype(BF16)
    widened = jnp.broadcast_to(scaled[:, None, :, None], (count_rows, edge, count_cols, edge))
    return widened.reshape(count_rows * edge, count_cols * edge)


def dot(left, right, dims):
    return lax.dot_general(left, right, ((dims[:1], dims[1:]), ((), ())), preferred_element_type=F32)


def layer_kernel(
    tok_ref, grad_ref, wgu_ref, wd_ref, inner_ref, outer_ref,
    lo_ref, ig_ref, gu_ref, dn_ref,
    act, part, opp_in, sum_in, share, outs, ring_in, rows_out, rows_in, acc, pair_out, pair_in,
    send_sem, recv_sem, pair_send, pair_recv,
):
    x = lax.axis_index("row")
    y = lax.axis_index("col")
    d = lax.axis_index("dp")
    z = d // 2
    k = lax.rem(d, 2)
    xr, xl, xo = lax.rem(x + 1, 4), lax.rem(x + 3, 4), lax.rem(x + 2, 4)
    x_right, x_left = (xr, y, d), (xl, y, d)
    y_right = (x, lax.rem(y + 1, 4), d)
    y_left = (x, lax.rem(y + 3, 4), d)
    y_far = (x, lax.rem(y + 2, 4), d)
    z_right = (x, y, lax.rem(z + 1, 8) * 2 + k)
    z_left = (x, y, lax.rem(z + 7, 8) * 2 + k)
    sibling = (x, y, z * 2 + 1 - k)
    unit = wd_ref.shape[0]
    full = part.shape[2]
    half = full // 2
    lo_half, hi_half = pl.ds(0, half), pl.ds(half, half)

    barrier = pltpu.get_barrier_semaphore()
    peers = (x_right, x_left, y_right, y_left, y_far, z_right, z_left, sibling)
    for peer in peers:
        pl.semaphore_signal(barrier, inc=1, device_id=peer, device_id_type=MESH)
    for c in range(CHUNKS):
        act[c, 0, 0, 0] = tok_ref[pl.ds(c * ROWS, ROWS), :]
        act[c, 0, 0, 1] = grad_ref[pl.ds(c * ROWS, ROWS), :]
    pl.semaphore_wait(barrier, len(peers))

    copies = {}

    def add(name, src, dst, peer, land=None):
        copies[name] = (len(copies), src, dst, peer, dst if land is None else land)

    for step in range(4):
        up_from, up_to = (0, 1, 3, 5)[step], (1, 3, 5, 7)[step]
        dn_from, dn_to = (0, 2, 4, 6)[step], (2, 4, 6, 7)[step]
        if step < 3:
            add(f"zp{step}", lambda c, a=up_from: act.at[c, 0, a], lambda c, a=up_to: act.at[c, 0, a], z_right)
            add(f"zm{step}", lambda c, a=dn_from: act.at[c, 0, a], lambda c, a=dn_to: act.at[c, 0, a], z_left)
        else:
            add("zp3", lambda c: act.at[c, 0, 5, 0], lambda c: act.at[c, 0, 7, 0], z_right)
            add("zm3", lambda c: act.at[c, 0, 6, 1], lambda c: act.at[c, 0, 7, 1], z_left)
    for g, (a, b) in enumerate(GROUPS):
        sl = pl.ds(a, b - a)
        add(f"yp{g}", lambda c, sl=sl: act.at[c, 0, sl], lambda c, sl=sl: act.at[c, 1, sl], y_right)
        add(f"ym{g}", lambda c, sl=sl: act.at[c, 0, sl], lambda c, sl=sl: act.at[c, 2, sl], y_left)
        add(f"yfp{g}", lambda c, sl=sl: act.at[c, 1, sl, 0], lambda c, sl=sl: act.at[c, 3, sl, 0], y_right)
        add(f"yfm{g}", lambda c, sl=sl: act.at[c, 2, sl, 1], lambda c, sl=sl: act.at[c, 3, sl, 1], y_left)
    add("xop", lambda c: part.at[c, xo, lo_half], lambda c: opp_in.at[c, 0], x_right)
    add("xom", lambda c: part.at[c, xo, hi_half], lambda c: opp_in.at[c, 1], x_left)
    add("xdp", lambda c: part.at[c, xr, hi_half], lambda c: sum_in.at[c, 0, hi_half], x_right)
    add("xdm", lambda c: part.at[c, xl, lo_half], lambda c: sum_in.at[c, 1, lo_half], x_left)
    add("xsp", lambda c: part.at[c, xr, lo_half], lambda c: sum_in.at[c, 0, lo_half], x_right)
    add("xsm", lambda c: part.at[c, xl, hi_half], lambda c: sum_in.at[c, 1, hi_half], x_left)
    add("xap", lambda c: share.at[c, x], lambda c: share.at[c, x], x_right, lambda c: share.at[c, xl])
    add("xam", lambda c: share.at[c, x], lambda c: share.at[c, x], x_left, lambda c: share.at[c, xr])
    add("xfp", lambda c: share.at[c, xl, lo_half], lambda c: share.at[c, xl, lo_half], x_right,
        lambda c: share.at[c, xo, lo_half])
    add("xfm", lambda c: share.at[c, xr, hi_half], lambda c: share.at[c, xr, hi_half], x_left,
        lambda c: share.at[c, xo, hi_half])
    first, last = pl.ds(0, 4), pl.ds(4, 4)
    add("rp0", lambda c: outs.at[c, 7, first], lambda c: ring_in.at[c, 0, 0, first], z_right)
    add("rm0", lambda c: outs.at[c, 7, last], lambda c: ring_in.at[c, 1, 0, last], z_left)
    for step in range(1, 4):
        a, b = (6, 4, 2)[step - 1], (5, 3, 1)[step - 1]
        add(f"rp{step}", lambda c, a=a: outs.at[c, a], lambda c, step=step: ring_in.at[c, 0, step], z_right)
        add(f"rm{step}", lambda c, b=b: outs.at[c, b], lambda c, step=step: ring_in.at[c, 1, step], z_left)
    add("tp", lambda c: rows_out.at[c, 2], lambda c: rows_in.at[c, 0], y_right)
    add("tm", lambda c: rows_out.at[c, 1], lambda c: rows_in.at[c, 1], y_left)
    add("tf", lambda c: rows_out.at[c, 3], lambda c: rows_in.at[c, 2], y_far)
    assert len(copies) == send_sem.shape[1]

    def describe(src, dst, c, index, peer):
        return pltpu.make_async_remote_copy(
            src_ref=src, dst_ref=dst, send_sem=send_sem.at[c, index], recv_sem=recv_sem.at[c, index],
            device_id=peer, device_id_type=MESH,
        )

    def start(c, *names):
        for name in names:
            index, src, dst, peer, land = copies[name]
            describe(src(c), dst(c), c, index, peer).start()

    def got(c, *names):
        for name in names:
            index, src, dst, peer, land = copies[name]
            describe(land(c), land(c), c, index, peer).wait_recv()

    def sent(c, *names):
        for name in names:
            index, src, dst, peer, land = copies[name]
            describe(src(c), dst(c), c, index, peer).wait_send()

    def gather(step, c):
        if step == 0:
            start(c, "zp0", "zm0", "yp0", "ym0")
        elif step == 1:
            got(c, "zp0", "zm0")
            start(c, "zp1", "zm1", "yp1", "ym1")
            got(c, "yp0", "ym0")
            start(c, "yfp0", "yfm0")
        elif step == 2:
            got(c, "zp1", "zm1")
            start(c, "zp2", "zm2", "yp2", "ym2")
        elif step == 3:
            got(c, "zp2", "zm2")
            start(c, "zp3", "zm3")
            got(c, "yp1", "ym1")
            start(c, "yfp1", "yfm1")
        elif step == 4:
            got(c, "zp3", "zm3")
            start(c, "yp3", "ym3")
            got(c, "yp2", "ym2")
            start(c, "yfp2", "yfm2")
        elif step == 5:
            got(c, "yp3", "ym3")
            start(c, "yfp3", "yfm3")
        else:
            for g in range(len(GROUPS)):
                got(c, f"yfp{g}", f"yfm{g}")

    def rows_of(c, first_y, count, which):
        return act[c, pl.ds(first_y, count), :, which].reshape(count * SLOTS * ROWS, -1)

    def project(c):
        @pl.loop(0, 2)
        def _(h):
            gu = dot(wgu_ref[...], rows_of(c, 2 * h, 2, 0), (1, 1)).astype(BF16)
            part[c, 2 * h, pl.ds(0, 2 * unit)] = gu[:, :128]
            part[c, 2 * h + 1, pl.ds(0, 2 * unit)] = gu[:, 128:]
            hg = dot(wd_ref[...], rows_of(c, 2 * h, 2, 1), (1, 1)).astype(BF16)
            part[c, 2 * h, pl.ds(2 * unit, unit)] = hg[:, :128]
            part[c, 2 * h + 1, pl.ds(2 * unit, unit)] = hg[:, 128:]

        start(c, "xop", "xom", "xdp", "xdm")

    tile = 112

    def middle_sums(c):
        got(c, "xop", "xom")

        @pl.loop(0, half // tile)
        def _(i):
            at = pl.ds(pl.multiple_of(i * tile, 16), tile)
            up = pl.ds(pl.multiple_of(half + i * tile, 16), tile)
            part[c, xr, at] = (part[c, xr, at].astype(F32) + opp_in[c, 0, at].astype(F32)).astype(BF16)
            part[c, xl, up] = (part[c, xl, up].astype(F32) + opp_in[c, 1, at].astype(F32)).astype(BF16)

        start(c, "xsp", "xsm")

    def gated(c):
        got(c, "xdp", "xdm", "xsp", "xsm")

        def total(at):
            return part[c, x, at].astype(F32) + sum_in[c, 0, at].astype(F32) + sum_in[c, 1, at].astype(F32)

        step = 64

        @pl.loop(0, unit // step)
        def _(i):
            at = pl.ds(pl.multiple_of(i * step, 16), step)
            at_up = pl.ds(pl.multiple_of(unit + i * step, 16), step)
            at_dn = pl.ds(pl.multiple_of(2 * unit + i * step, 16), step)
            gate, up, grad = total(at), total(at_up), total(at_dn)
            sig = 1.0 / (1.0 + jnp.exp(-gate))
            act_gate = gate * sig
            share[c, x, at_dn] = (act_gate * up).astype(BF16)
            share[c, x, at] = (grad * up * sig * (1.0 + gate * (1.0 - sig))).astype(BF16)
            share[c, x, at_up] = (grad * act_gate).astype(BF16)

        start(c, "xap", "xam")

    def forward_shares(c):
        got(c, "xap", "xam")
        start(c, "xfp", "xfm")

    def joined(c, rows, first_part, count):
        return jnp.concatenate([share[c, first_part + i, rows] for i in range(count)], axis=1)

    def outputs(c):
        got(c, "xfp", "xfm")

        @pl.loop(0, 2)
        def _(h):
            hidden = joined(c, pl.ds(2 * unit, unit), 2 * h, 2)
            lo = dot(hidden, wd_ref[...], (0, 0)).astype(BF16).reshape(2, SLOTS, ROWS, -1)
            outs[c, :, 2 * h] = lo[0]
            outs[c, :, 2 * h + 1] = lo[1]
            backs = joined(c, pl.ds(0, 2 * unit), 2 * h, 2)
            ig = dot(backs, wgu_ref[...], (0, 0)).astype(BF16).reshape(2, SLOTS, ROWS, -1)
            outs[c, :, 4 + 2 * h] = ig[0]
            outs[c, :, 5 + 2 * h] = ig[1]

        start(c, "rp0", "rm0")

    def ring(step, c):
        got(c, f"rp{step - 1}", f"rm{step - 1}")
        if step < 4:
            a, b = (6, 4, 2)[step - 1], (5, 3, 1)[step - 1]

            def bump(slot, way, i):
                outs[c, slot, i] = (outs[c, slot, i].astype(F32) + ring_in[c, way, step - 1, i].astype(F32)).astype(BF16)

            if step == 1:

                @pl.loop(0, 4)
                def _(i):
                    bump(a, 0, i)
                    bump(b, 1, i + 4)
            else:

                @pl.loop(0, 8)
                def _(i):
                    bump(a, 0, i)
                    bump(b, 1, i)

            start(c, f"rp{step}", f"rm{step}")
        else:
            for dest in range(1, 4):
                for which in range(2):
                    rows_out[c, dest, which] = own_sum(c, which * 4 + dest).astype(BF16)
            start(c, "tp", "tm", "tf")

    def own_sum(c, i):
        return outs[c, 0, i].astype(F32) + ring_in[c, 0, 3, i].astype(F32) + ring_in[c, 1, 3, i].astype(F32)

    def finish_rows(c):
        got(c, "tp", "tm", "tf")
        at = pl.ds(pl.multiple_of(c * ROWS, ROWS), ROWS)
        for which, ref in ((0, lo_ref), (1, ig_ref)):
            total = own_sum(c, which * 4)
            for i in range(3):
                total = total + rows_in[c, i, which].astype(F32)
            ref[at, :] = total.astype(BF16)

    width = 256

    def weight_grads(c):
        @pl.loop(0, acc.shape[1] // width)
        def _(n):
            lanes = pl.ds(pl.multiple_of(n * width, width), width)
            tokens = act[c, :, :, 0, :, lanes].reshape(4 * SLOTS * ROWS, width)
            grads = act[c, :, :, 1, :, lanes].reshape(4 * SLOTS * ROWS, width)
            gu = dot(joined(c, pl.ds(0, 2 * unit), 0, 4), tokens, (1, 0))
            dn = dot(joined(c, pl.ds(2 * unit, unit), 0, 4), grads, (1, 0))
            acc[pl.ds(0, 2 * unit), lanes] += gu
            acc[pl.ds(2 * unit, unit), lanes] += dn

    own = unit // 2

    def pair_copy():
        return pltpu.make_async_remote_copy(
            src_ref=pair_out, dst_ref=pair_in, send_sem=pair_send, recv_sem=pair_recv,
            device_id=sibling, device_id_type=MESH,
        )

    def own_rows(i, which):
        return pl.ds(pl.multiple_of(i * unit + which * own, 32), own)

    def pair_start():
        for i in range(3):
            pair_out[i] = acc[own_rows(i, 1 - k), :].astype(BF16)
        pair_copy().start()

    def pair_finish():
        pair_copy().wait_recv()
        mine = pl.ds(pl.multiple_of(k * own, 32), own)
        for i in range(3):
            total = acc[own_rows(i, k), :] + pair_in[i].astype(F32)
            if i < 2:
                gu_ref[i] = (total * inner_ref[mine, :].astype(F32)).astype(BF16)
            else:
                dn_ref[...] = (total * outer_ref[mine, :].astype(F32)).astype(BF16)

    acc[...] = jnp.zeros_like(acc)

    @pl.loop(0, CHUNKS + 2)
    def _(s):
        ahead, now, behind = s, s - 1, s - 2

        def when_ahead(f, *a):
            pl.when(ahead < CHUNKS)(lambda: f(*a, ahead))

        def when_now(f, *a):
            pl.when((now >= 0) & (now < CHUNKS))(lambda: f(*a, now))

        def when_behind(f, *a):
            pl.when(behind >= 0)(lambda: f(*a, behind))

        def at_end(f):
            pl.when(s == CHUNKS + 1)(f)

        when_ahead(gather, 0)
        when_now(project)
        when_behind(ring, 1)
        when_ahead(gather, 1)
        when_behind(weight_grads)
        at_end(pair_start)
        when_now(middle_sums)
        when_behind(ring, 2)
        when_ahead(gather, 2)
        when_now(gated)
        when_behind(ring, 3)
        at_end(pair_finish)
        when_ahead(gather, 3)
        when_now(forward_shares)
        when_behind(ring, 4)
        when_ahead(gather, 4)
        when_ahead(gather, 5)
        when_now(outputs)
        when_behind(finish_rows)
        when_ahead(gather, 6)
        pl.when(behind >= 0)(lambda: sent(behind, *copies))

    pair_copy().wait_send()


def on_device(tokens_in, out_grad, gate_weight, up_weight, down_weight, inner_mask, outer_mask):
    edge = gate_weight.shape[0] // inner_mask.shape[0]
    features, width = gate_weight.shape
    chips = lax.axis_size("dp") // 2
    unit = width // chips
    own = unit // 2
    offset = lax.axis_index("dp") // 2 * unit
    inner_slice = lax.dynamic_slice_in_dim(expand_blocks(inner_mask.T, edge), offset, unit, 0)
    outer_slice = lax.dynamic_slice_in_dim(expand_blocks(outer_mask, edge), offset, unit, 0)
    gate_eff = lax.dynamic_slice_in_dim(gate_weight, offset, unit, 1).T * inner_slice
    up_eff = lax.dynamic_slice_in_dim(up_weight, offset, unit, 1).T * inner_slice
    down_eff = lax.dynamic_slice_in_dim(down_weight, offset, unit, 0) * outer_slice
    joined = jnp.concatenate([gate_eff, up_eff], axis=0)
    rows = tokens_in.shape[0]
    full = 3 * unit
    copies = 45
    vmem = pl.BlockSpec(memory_space=pltpu.VMEM)
    layer_out, input_grad, gate_up, down_grad = pl.pallas_call(
        layer_kernel,
        name="layer",
        out_shape=(
            jax.ShapeDtypeStruct((rows, features), BF16),
            jax.ShapeDtypeStruct((rows, features), BF16),
            jax.ShapeDtypeStruct((2, own, features), BF16),
            jax.ShapeDtypeStruct((own, features), BF16),
        ),
        in_specs=[vmem] * 6,
        out_specs=(vmem,) * 4,
        scratch_shapes=[
            pltpu.VMEM((CHUNKS, 4, SLOTS, 2, ROWS, features), BF16),
            pltpu.VMEM((CHUNKS, 4, full, 128), BF16),
            pltpu.VMEM((CHUNKS, 2, full // 2, 128), BF16),
            pltpu.VMEM((CHUNKS, 2, full, 128), BF16),
            pltpu.VMEM((CHUNKS, 4, full, 128), BF16),
            pltpu.VMEM((CHUNKS, SLOTS, 8, ROWS, features), BF16),
            pltpu.VMEM((CHUNKS, 2, 4, 8, ROWS, features), BF16),
            pltpu.VMEM((CHUNKS, 4, 2, ROWS, features), BF16),
            pltpu.VMEM((CHUNKS, 3, 2, ROWS, features), BF16),
            pltpu.VMEM((full, features), F32),
            pltpu.VMEM((3, own, features), BF16),
            pltpu.VMEM((3, own, features), BF16),
            pltpu.SemaphoreType.DMA((CHUNKS, copies)),
            pltpu.SemaphoreType.DMA((CHUNKS, copies)),
            pltpu.SemaphoreType.DMA,
            pltpu.SemaphoreType.DMA,
        ],
        compiler_params=pltpu.CompilerParams(
            collective_id=0, has_side_effects=True, vmem_limit_bytes=58 * 2**20
        ),
    )(tokens_in, out_grad, joined, down_eff, inner_slice, outer_slice)
    return (layer_out, input_grad, gate_up[0].T, gate_up[1].T, down_grad)


def solution(mesh):
    placed = (
        P(("col", "dp"), "row"),
        P(("col", "dp"), "row"),
        P("row", "col"),
        P("row", "col"),
        P("col", "row"),
        P("row", "col"),
        P("col", "row"),
    )
    return jax.shard_map(
        on_device,
        mesh=mesh,
        in_specs=placed,
        out_specs=(
            P(("col", "dp"), "row"),
            P(("col", "dp"), "row"),
            P("row", ("col", "dp")),
            P("row", ("col", "dp")),
            P(("col", "dp"), "row"),
        ),
        check_vma=False,
    )
```

```python
import jax
import jax.numpy as jnp
from jax import lax
from jax.experimental import pallas as pl
from jax.experimental.pallas import tpu as pltpu
from jax.sharding import PartitionSpec as P

MESH = pl.DeviceIdType.MESH
F32 = jnp.float32
BF16 = jnp.bfloat16
CHUNKS = 3
ROWS = 16
SLOTS = 8
EDGE = 128
GRAIN = 32
WINDOW = 512
GROUPS = ((0, 1), (1, 3), (3, 5), (5, 8))
COPIES = 64


def dot(left, right, dims):
    return lax.dot_general(left, right, ((dims[:1], dims[1:]), ((), ())), preferred_element_type=F32)


def layer_kernel(
    tok_ref, grad_ref, gate_hbm, up_hbm, down_hbm, inner_ref, outer_ref,
    lo_ref, ig_ref, gate_ref, up_ref, down_ref,
    act, part, opp_in, sum_in, share, outs, ring_in, rows_out, rows_in, acc, pair_out, pair_in,
    wgu, wd, window, turned,
    send_sem, recv_sem, pair_send, pair_recv, load_sem,
):
    x = lax.axis_index("row")
    y = lax.axis_index("col")
    d = lax.axis_index("dp")
    z = d // 2
    k = lax.rem(d, 2)
    xr, xl, xo = lax.rem(x + 1, 4), lax.rem(x + 3, 4), lax.rem(x + 2, 4)
    x_right, x_left = (xr, y, d), (xl, y, d)
    y_right = (x, lax.rem(y + 1, 4), d)
    y_left = (x, lax.rem(y + 3, 4), d)
    y_far = (x, lax.rem(y + 2, 4), d)
    z_right = (x, y, lax.rem(z + 1, 8) * 2 + k)
    z_left = (x, y, lax.rem(z + 7, 8) * 2 + k)
    sibling = (x, y, z * 2 + 1 - k)
    own = wd.shape[1]
    unit = 2 * own
    full = part.shape[3]
    half = full // 2
    lo_half, hi_half = pl.ds(0, half), pl.ds(half, half)

    base = pl.multiple_of((7 * z) // 2 * EDGE, EDGE)
    loads = [
        pltpu.make_async_copy(gate_hbm.at[:, pl.ds(base, WINDOW)], window.at[0], load_sem.at[0]),
        pltpu.make_async_copy(up_hbm.at[:, pl.ds(base, WINDOW)], window.at[1], load_sem.at[1]),
    ]
    for h in range(2):
        rows = pl.ds(pl.multiple_of(z * unit + h * own, GRAIN), own)
        loads.append(pltpu.make_async_copy(down_hbm.at[rows, :], wd.at[h], load_sem.at[2 + h]))
    for load in loads:
        load.start()

    barrier = pltpu.get_barrier_semaphore()
    peers = (x_right, x_left, y_right, y_left, y_far, z_right, z_left, sibling)
    for peer in peers:
        pl.semaphore_signal(barrier, inc=1, device_id=peer, device_id_type=MESH)
    for c in range(CHUNKS):
        act[c, 0, 0, 0] = tok_ref[pl.ds(c * ROWS, ROWS), :]
        act[c, 0, 0, 1] = grad_ref[pl.ds(c * ROWS, ROWS), :]
    pl.semaphore_wait(barrier, len(peers))

    copies = {}

    def add(name, src, dst, peer, land=None):
        copies[name] = (len(copies), src, dst, peer, dst if land is None else land)

    for step in range(3):
        up_from, up_to = (0, 1, 3)[step], (1, 3, 5)[step]
        dn_from, dn_to = (0, 2, 4)[step], (2, 4, 6)[step]
        add(f"zp{step}", lambda c, a=up_from: act.at[c, 0, a], lambda c, a=up_to: act.at[c, 0, a], z_right)
        add(f"zm{step}", lambda c, a=dn_from: act.at[c, 0, a], lambda c, a=dn_to: act.at[c, 0, a], z_left)
    add("zp3", lambda c: act.at[c, 0, 5, 0], lambda c: act.at[c, 0, 7, 0], z_right)
    add("zm3", lambda c: act.at[c, 0, 6, 1], lambda c: act.at[c, 0, 7, 1], z_left)
    for g, (a, b) in enumerate(GROUPS):
        sl = pl.ds(a, b - a)
        add(f"yp{g}", lambda c, sl=sl: act.at[c, 0, sl], lambda c, sl=sl: act.at[c, 1, sl], y_right)
        add(f"ym{g}", lambda c, sl=sl: act.at[c, 0, sl], lambda c, sl=sl: act.at[c, 2, sl], y_left)
        add(f"yfp{g}", lambda c, sl=sl: act.at[c, 1, sl, 0], lambda c, sl=sl: act.at[c, 3, sl, 0], y_right)
        add(f"yfm{g}", lambda c, sl=sl: act.at[c, 2, sl, 1], lambda c, sl=sl: act.at[c, 3, sl, 1], y_left)
    for h in range(2):
        add(f"xop{h}", lambda c, h=h: part.at[c, h, xo, lo_half], lambda c, h=h: opp_in.at[c, h, 0], x_right)
        add(f"xom{h}", lambda c, h=h: part.at[c, h, xo, hi_half], lambda c, h=h: opp_in.at[c, h, 1], x_left)
        add(f"xdp{h}", lambda c, h=h: part.at[c, h, xr, hi_half], lambda c, h=h: sum_in.at[c, h, 0, hi_half], x_right)
        add(f"xdm{h}", lambda c, h=h: part.at[c, h, xl, lo_half], lambda c, h=h: sum_in.at[c, h, 1, lo_half], x_left)
        add(f"xsp{h}", lambda c, h=h: part.at[c, h, xr, lo_half], lambda c, h=h: sum_in.at[c, h, 0, lo_half], x_right)
        add(f"xsm{h}", lambda c, h=h: part.at[c, h, xl, hi_half], lambda c, h=h: sum_in.at[c, h, 1, hi_half], x_left)
        add(f"xap{h}", lambda c, h=h: share.at[c, h, x], lambda c, h=h: share.at[c, h, x], x_right,
            lambda c, h=h: share.at[c, h, xl])
        add(f"xam{h}", lambda c, h=h: share.at[c, h, x], lambda c, h=h: share.at[c, h, x], x_left,
            lambda c, h=h: share.at[c, h, xr])
        add(f"xfp{h}", lambda c, h=h: share.at[c, h, xl, lo_half], lambda c, h=h: share.at[c, h, xl, lo_half], x_right,
            lambda c, h=h: share.at[c, h, xo, lo_half])
        add(f"xfm{h}", lambda c, h=h: share.at[c, h, xr, hi_half], lambda c, h=h: share.at[c, h, xr, hi_half], x_left,
            lambda c, h=h: share.at[c, h, xo, hi_half])
    up_slots, dn_slots = (7, 6, 4, 2), (7, 5, 3, 1)
    for which in range(2):
        block = pl.ds(which * 4, 4)
        for way in range(2):
            for step in range(0 if which == way else 1, 4):
                slot = (up_slots, dn_slots)[way][step]
                add(f"r{way}{which}{step}", lambda c, s=slot, block=block: outs.at[c, s, block],
                    lambda c, w=way, s=step, block=block: ring_in.at[c, w, s, block], (z_right, z_left)[way])
        add(f"tp{which}", lambda c, w=which: rows_out.at[c, 2, w], lambda c, w=which: rows_in.at[c, 0, w], y_right)
        add(f"tm{which}", lambda c, w=which: rows_out.at[c, 1, w], lambda c, w=which: rows_in.at[c, 1, w], y_left)
        add(f"tf{which}", lambda c, w=which: rows_out.at[c, 3, w], lambda c, w=which: rows_in.at[c, 2, w], y_far)
    assert len(copies) == send_sem.shape[1], len(copies)

    def describe(src, dst, c, index, peer):
        return pltpu.make_async_remote_copy(
            src_ref=src, dst_ref=dst, send_sem=send_sem.at[c, index], recv_sem=recv_sem.at[c, index],
            device_id=peer, device_id_type=MESH,
        )

    def start(c, *names):
        for name in names:
            index, src, dst, peer, land = copies[name]
            describe(src(c), dst(c), c, index, peer).start()

    def got(c, *names):
        for name in names:
            index, src, dst, peer, land = copies[name]
            describe(land(c), land(c), c, index, peer).wait_recv()

    def sent(c, *names):
        for name in names:
            index, src, dst, peer, land = copies[name]
            describe(src(c), dst(c), c, index, peer).wait_send()

    def mask_row(i):
        return (14 * z + i) // 4

    def load_gate_up(i):
        loads[i].wait()

        @pl.loop(0, tok_ref.shape[1] // EDGE)
        def _(f):
            at = pl.ds(pl.multiple_of(f * EDGE, EDGE), EDGE)
            turned[...] = window[i, at, :].T
            for g in range(14):
                rows = pl.ds(pl.multiple_of(lax.rem(z, 2) * 64 + g * GRAIN, GRAIN), GRAIN)
                keep = inner_ref[f, mask_row(g)].astype(F32)
                into = pl.ds(i * own + g % 7 * GRAIN, GRAIN)
                wgu[g // 7, into, at] = (turned[rows, :].astype(F32) * keep).astype(BF16)

    def load_down():
        loads[2].wait()
        loads[3].wait()

        @pl.loop(0, tok_ref.shape[1] // EDGE)
        def _(f):
            at = pl.ds(pl.multiple_of(f * EDGE, EDGE), EDGE)
            for g in range(14):
                rows = pl.ds(g % 7 * GRAIN, GRAIN)
                keep = outer_ref[f, mask_row(g)].astype(F32)
                wd[g // 7, rows, at] = (wd[g // 7, rows, at].astype(F32) * keep).astype(BF16)

    def gather(step, c):
        if step == 0:
            start(c, "zp0", "zm0", "yp0", "ym0")
        elif step == 1:
            got(c, "zp0", "zm0")
            start(c, "zp1", "zm1", "yp1", "ym1")
            got(c, "yp0", "ym0")
            start(c, "yfp0", "yfm0")
        elif step == 2:
            got(c, "zp1", "zm1")
            start(c, "zp2", "zm2", "yp2", "ym2")
        elif step == 3:
            got(c, "zp2", "zm2")
            start(c, "zp3", "zm3")
            got(c, "yp1", "ym1")
            start(c, "yfp1", "yfm1")
        elif step == 4:
            got(c, "zp3", "zm3")
            start(c, "yp3", "ym3")
            got(c, "yp2", "ym2")
            start(c, "yfp2", "yfm2")
        elif step == 5:
            got(c, "yp3", "ym3")
            start(c, "yfp3", "yfm3")
        else:
            for g in range(len(GROUPS)):
                got(c, f"yfp{g}", f"yfm{g}")

    def rows_of(c, first_y, count, which):
        return act[c, pl.ds(first_y, count), :, which].reshape(count * SLOTS * ROWS, -1)

    def project(h, c):
        @pl.loop(0, 2)
        def _(p):
            gu = dot(wgu[h], rows_of(c, 2 * p, 2, 0), (1, 1)).astype(BF16)
            part[c, h, 2 * p, pl.ds(0, unit)] = gu[:, :128]
            part[c, h, 2 * p + 1, pl.ds(0, unit)] = gu[:, 128:]
            hg = dot(wd[h], rows_of(c, 2 * p, 2, 1), (1, 1)).astype(BF16)
            part[c, h, 2 * p, pl.ds(unit, own)] = hg[:, :128]
            part[c, h, 2 * p + 1, pl.ds(unit, own)] = hg[:, 128:]

        start(c, f"xop{h}", f"xom{h}", f"xdp{h}", f"xdm{h}")

    tile = 112

    def middle_sums(h, c):
        got(c, f"xop{h}", f"xom{h}")

        @pl.loop(0, half // tile)
        def _(i):
            at = pl.ds(pl.multiple_of(i * tile, 16), tile)
            up = pl.ds(pl.multiple_of(half + i * tile, 16), tile)
            part[c, h, xr, at] = (part[c, h, xr, at].astype(F32) + opp_in[c, h, 0, at].astype(F32)).astype(BF16)
            part[c, h, xl, up] = (part[c, h, xl, up].astype(F32) + opp_in[c, h, 1, at].astype(F32)).astype(BF16)

        start(c, f"xsp{h}", f"xsm{h}")

    def gated(h, c):
        got(c, f"xdp{h}", f"xdm{h}", f"xsp{h}", f"xsm{h}")

        def total(at):
            return part[c, h, x, at].astype(F32) + sum_in[c, h, 0, at].astype(F32) + sum_in[c, h, 1, at].astype(F32)

        @pl.loop(0, own // GRAIN)
        def _(i):
            at = pl.ds(pl.multiple_of(i * GRAIN, GRAIN), GRAIN)
            at_up = pl.ds(pl.multiple_of(own + i * GRAIN, GRAIN), GRAIN)
            at_dn = pl.ds(pl.multiple_of(unit + i * GRAIN, GRAIN), GRAIN)
            gate, up, grad = total(at), total(at_up), total(at_dn)
            sig = 1.0 / (1.0 + jnp.exp(-gate))
            act_gate = gate * sig
            share[c, h, x, at_dn] = (act_gate * up).astype(BF16)
            share[c, h, x, at] = (grad * up * sig * (1.0 + gate * (1.0 - sig))).astype(BF16)
            share[c, h, x, at_up] = (grad * act_gate).astype(BF16)

        start(c, f"xap{h}", f"xam{h}")

    def forward_shares(h, c):
        got(c, f"xap{h}", f"xam{h}")
        start(c, f"xfp{h}", f"xfm{h}")

    def joined(c, h, rows, first_part, count):
        return jnp.concatenate([share[c, h, first_part + i, rows] for i in range(count)], axis=1)

    def both(c, rows, first_part, count):
        return jnp.concatenate([joined(c, h, rows, first_part, count) for h in range(2)], axis=0)

    def outputs(c):
        got(c, "xfp0", "xfm0", "xfp1", "xfm1")
        for which in range(2):

            @pl.loop(0, 2)
            def _(p):
                if which == 0:
                    left, right = both(c, pl.ds(unit, own), 2 * p, 2), wd[...].reshape(unit, -1)
                else:
                    left, right = both(c, pl.ds(0, unit), 2 * p, 2), wgu[...].reshape(2 * unit, -1)
                done = dot(left, right, (0, 0)).astype(BF16).reshape(2, SLOTS, ROWS, -1)
                outs[c, :, 4 * which + 2 * p] = done[0]
                outs[c, :, 4 * which + 2 * p + 1] = done[1]

            start(c, f"r{which}{which}0")
            start(c, f"r{1 - which}{which}1")

    def ring(which_long, step, c):
        for way in range(2):
            which = way if which_long else 1 - way
            got(c, f"r{way}{which}{step - 1}")
            slot = (up_slots, dn_slots)[way][step]

            @pl.loop(4 * which, 4 * which + 4)
            def _(i):
                outs[c, slot, i] = (outs[c, slot, i].astype(F32) + ring_in[c, way, step - 1, i].astype(F32)).astype(BF16)

            start(c, f"r{way}{which}{step}")

    def own_sum(c, i):
        return outs[c, 0, i].astype(F32) + ring_in[c, 0, 3, i].astype(F32) + ring_in[c, 1, 3, i].astype(F32)

    def leave(c):
        for which in range(2):
            got(c, f"r0{which}3", f"r1{which}3")
            for dest in range(1, 4):
                rows_out[c, dest, which] = own_sum(c, which * 4 + dest).astype(BF16)
            start(c, f"tp{which}", f"tm{which}", f"tf{which}")

    def finish_rows(c):
        at = pl.ds(pl.multiple_of(c * ROWS, ROWS), ROWS)
        for which, ref in ((0, lo_ref), (1, ig_ref)):
            got(c, f"tp{which}", f"tm{which}", f"tf{which}")
            total = own_sum(c, which * 4)
            for i in range(3):
                total = total + rows_in[c, i, which].astype(F32)
            ref[at, :] = total.astype(BF16)

    width = 256

    def weight_grads(c):
        @pl.loop(0, acc.shape[2] // width)
        def _(n):
            lanes = pl.ds(pl.multiple_of(n * width, width), width)
            tokens = act[c, :, :, 0, :, lanes].reshape(4 * SLOTS * ROWS, width)
            grads = act[c, :, :, 1, :, lanes].reshape(4 * SLOTS * ROWS, width)
            for h in range(2):
                acc[h, pl.ds(0, unit), lanes] += dot(joined(c, h, pl.ds(0, unit), 0, 4), tokens, (1, 0))
                acc[h, pl.ds(unit, own), lanes] += dot(joined(c, h, pl.ds(unit, own), 0, 4), grads, (1, 0))

    def pair_copy():
        return pltpu.make_async_remote_copy(
            src_ref=pair_out, dst_ref=pair_in, send_sem=pair_send, recv_sem=pair_recv,
            device_id=sibling, device_id_type=MESH,
        )

    def pair_start():
        pair_out[...] = acc[1 - k].astype(BF16)
        pair_copy().start()

    def pair_finish():
        pair_copy().wait_recv()

        @pl.loop(0, tok_ref.shape[1] // EDGE)
        def _(f):
            at = pl.ds(pl.multiple_of(f * EDGE, EDGE), EDGE)
            for i, ref in enumerate((gate_ref, up_ref, down_ref)):
                pieces = []
                for g in range(7):
                    rows = pl.ds(i * own + g * GRAIN, GRAIN)
                    block = mask_row(7 * k + g)
                    keep = (inner_ref if i < 2 else outer_ref)[f, block].astype(F32)
                    pieces.append((acc[k, rows, at] + pair_in[rows, at].astype(F32)) * keep)
                ref[:, at] = jnp.concatenate(pieces, axis=0).astype(BF16)

    gather(0, 0)
    acc[...] = jnp.zeros_like(acc)

    @pl.loop(0, CHUNKS + 2)
    def _(s):
        ahead, now, behind = s, s - 1, s - 2

        def when_ahead(f, *a):
            pl.when(ahead < CHUNKS)(lambda: f(*a, ahead))

        def when_now(f, *a):
            pl.when((now >= 0) & (now < CHUNKS))(lambda: f(*a, now))

        def when_behind(f, *a):
            pl.when(behind >= 0)(lambda: f(*a, behind))

        def at_end(f):
            pl.when(s == CHUNKS + 1)(f)

        def at_first(f, *a):
            pl.when(s == 0)(lambda: f(*a))

        when_ahead(gather, 1)
        at_first(load_gate_up, 0)
        when_now(middle_sums, 0)
        when_ahead(gather, 2)
        at_first(load_gate_up, 1)
        when_behind(ring, True, 1)
        when_ahead(gather, 3)
        when_now(middle_sums, 1)
        when_behind(ring, False, 2)
        when_ahead(gather, 4)
        at_first(load_down)
        when_now(gated, 0)
        when_behind(ring, True, 2)
        when_now(gated, 1)
        when_ahead(gather, 5)
        when_behind(ring, False, 3)
        when_behind(weight_grads)
        at_end(pair_start)
        when_now(forward_shares, 0)
        when_behind(ring, True, 3)
        when_now(forward_shares, 1)
        at_end(pair_finish)
        when_ahead(gather, 6)
        pl.when(s + 1 < CHUNKS)(lambda: gather(0, s + 1))
        when_ahead(project, 0)
        when_ahead(project, 1)
        when_behind(leave)
        when_now(outputs)
        when_behind(finish_rows)
        pl.when(behind >= 0)(lambda: sent(behind, *copies))

    pair_copy().wait_send()


def on_device(tokens_in, out_grad, gate_weight, up_weight, down_weight, inner_mask, outer_mask):
    features, width = gate_weight.shape
    own = width // lax.axis_size("dp")
    rows = tokens_in.shape[0]
    full = 3 * own
    vmem = pl.BlockSpec(memory_space=pltpu.VMEM)
    smem = pl.BlockSpec(memory_space=pltpu.SMEM)
    anywhere = pl.BlockSpec(memory_space=pl.ANY)
    layer_out, input_grad, gate_grad, up_grad, down_grad = pl.pallas_call(
        layer_kernel,
        name="layer",
        out_shape=(
            jax.ShapeDtypeStruct((rows, features), BF16),
            jax.ShapeDtypeStruct((rows, features), BF16),
            jax.ShapeDtypeStruct((own, features), BF16),
            jax.ShapeDtypeStruct((own, features), BF16),
            jax.ShapeDtypeStruct((own, features), BF16),
        ),
        in_specs=[vmem, vmem, anywhere, anywhere, anywhere, smem, smem],
        out_specs=(vmem,) * 5,
        scratch_shapes=[
            pltpu.VMEM((CHUNKS, 4, SLOTS, 2, ROWS, features), BF16),
            pltpu.VMEM((CHUNKS, 2, 4, full, 128), BF16),
            pltpu.VMEM((CHUNKS, 2, 2, full // 2, 128), BF16),
            pltpu.VMEM((CHUNKS, 2, 2, full, 128), BF16),
            pltpu.VMEM((CHUNKS, 2, 4, full, 128), BF16),
            pltpu.VMEM((CHUNKS, SLOTS, 8, ROWS, features), BF16),
            pltpu.VMEM((CHUNKS, 2, 4, 8, ROWS, features), BF16),
            pltpu.VMEM((CHUNKS, 4, 2, ROWS, features), BF16),
            pltpu.VMEM((CHUNKS, 3, 2, ROWS, features), BF16),
            pltpu.VMEM((2, full, features), F32),
            pltpu.VMEM((full, features), BF16),
            pltpu.VMEM((full, features), BF16),
            pltpu.VMEM((2, 2 * own, features), BF16),
            pltpu.VMEM((2, own, features), BF16),
            pltpu.VMEM((2, features, WINDOW), BF16),
            pltpu.VMEM((WINDOW, EDGE), BF16),
            pltpu.SemaphoreType.DMA((CHUNKS, COPIES)),
            pltpu.SemaphoreType.DMA((CHUNKS, COPIES)),
            pltpu.SemaphoreType.DMA,
            pltpu.SemaphoreType.DMA,
            pltpu.SemaphoreType.DMA((4,)),
        ],
        compiler_params=pltpu.CompilerParams(
            collective_id=0, has_side_effects=True, vmem_limit_bytes=58 * 2**20
        ),
    )(tokens_in, out_grad, gate_weight, up_weight, down_weight, inner_mask, outer_mask.T)
    return (layer_out, input_grad, gate_grad.T, up_grad.T, down_grad)


def solution(mesh):
    placed = (
        P(("col", "dp"), "row"),
        P(("col", "dp"), "row"),
        P("row", "col"),
        P("row", "col"),
        P("col", "row"),
        P("row", "col"),
        P("col", "row"),
    )
    return jax.shard_map(
        on_device,
        mesh=mesh,
        in_specs=placed,
        out_specs=(
            P(("col", "dp"), "row"),
            P(("col", "dp"), "row"),
            P("row", ("col", "dp")),
            P("row", ("col", "dp")),
            P(("col", "dp"), "row"),
        ),
        check_vma=False,
    )
```

```python
import jax
import jax.numpy as jnp
from jax import lax
from jax.experimental import pallas as pl
from jax.experimental.pallas import tpu as pltpu
from jax.sharding import PartitionSpec as P

MESH = pl.DeviceIdType.MESH
F32 = jnp.float32
BF16 = jnp.bfloat16
CHUNKS = 3
ROWS = 16
SLOTS = 8
EDGE = 128
GRAIN = 32
WINDOW = 512
GROUPS = ((0, 1), (1, 3), (3, 5), (5, 8))
SUM_GROUPS = ((7, 8), (5, 7), (3, 5), (0, 3))
COPIES = 92


def dot(left, right, dims):
    return lax.dot_general(left, right, ((dims[:1], dims[1:]), ((), ())), preferred_element_type=F32)


def layer_kernel(
    tok_ref, grad_ref, gate_hbm, up_hbm, down_hbm, inner_ref, outer_ref,
    lo_ref, ig_ref, gate_ref, up_ref, down_ref,
    act, gact, part, opp_in, sum_in, share, outs, gouts, ring_in, gring_in, col_in, rows_out, rows_in, acc, pair_out, pair_in,
    wgu, wd, window, turned,
    send_sem, recv_sem, pair_send, pair_recv, load_sem,
):
    x = lax.axis_index("row")
    y = lax.axis_index("col")
    d = lax.axis_index("dp")
    z = d // 2
    k = lax.rem(d, 2)
    xr, xl, xo = lax.rem(x + 1, 4), lax.rem(x + 3, 4), lax.rem(x + 2, 4)
    x_right, x_left = (xr, y, d), (xl, y, d)
    y_right = (x, lax.rem(y + 1, 4), d)
    y_left = (x, lax.rem(y + 3, 4), d)
    y_far = (x, lax.rem(y + 2, 4), d)
    z_right = (x, y, lax.rem(z + 1, 8) * 2 + k)
    z_left = (x, y, lax.rem(z + 7, 8) * 2 + k)
    sibling = (x, y, z * 2 + 1 - k)
    own = wd.shape[1]
    unit = 2 * own
    full = part.shape[3]
    half = full // 2
    lo_half, hi_half = pl.ds(0, half), pl.ds(half, half)

    base = pl.multiple_of((7 * z) // 2 * EDGE, EDGE)
    loads = [
        pltpu.make_async_copy(gate_hbm.at[:, pl.ds(base, WINDOW)], window.at[0], load_sem.at[0]),
        pltpu.make_async_copy(up_hbm.at[:, pl.ds(base, WINDOW)], window.at[1], load_sem.at[1]),
    ]
    for h in range(2):
        rows = pl.ds(pl.multiple_of(z * unit + h * own, GRAIN), own)
        loads.append(pltpu.make_async_copy(down_hbm.at[rows, :], wd.at[h], load_sem.at[2 + h]))
    for load in loads:
        load.start()

    barrier = pltpu.get_barrier_semaphore()
    peers = (x_right, x_left, y_right, y_left, y_far, z_right, z_left, sibling)
    for peer in peers:
        pl.semaphore_signal(barrier, inc=1, device_id=peer, device_id_type=MESH)
    for c in range(CHUNKS):
        act[c, 0, 0] = tok_ref[pl.ds(c * ROWS, ROWS), :]
        gact[c, 0, 0] = grad_ref[pl.ds(c * ROWS, ROWS), :]
    pl.semaphore_wait(barrier, len(peers))

    copies = {}

    def add(name, src, dst, peer, land=None):
        copies[name] = (len(copies), src, dst, peer, dst if land is None else land)

    hops = (("p", (0, 1, 3, 5), (1, 3, 5, 7), z_right), ("m", (0, 2, 4, 6), (2, 4, 6, 7), z_left))
    for way, (letter, sources, targets, peer) in enumerate(hops):
        for step in range(4 if way == 0 else 3):
            add(f"z{letter}{step}", lambda c, a=sources[step]: act.at[c, 0, a], lambda c, a=targets[step]: act.at[c, 0, a], peer)
        for j in range(2):
            pair = pl.ds(2 * j, 2)
            for step in range(4 if way == j else 3):
                add(f"g{letter}{j}{step}", lambda c, a=sources[step], pair=pair: gact.at[c, a, pair],
                    lambda c, a=targets[step], pair=pair: gact.at[c, a, pair], peer)
    for g, (a, b) in enumerate(GROUPS):
        sl = pl.ds(a, b - a)
        add(f"yp{g}", lambda c, sl=sl: act.at[c, 0, sl], lambda c, sl=sl: act.at[c, 1, sl], y_right)
        add(f"ym{g}", lambda c, sl=sl: act.at[c, 0, sl], lambda c, sl=sl: act.at[c, 2, sl], y_left)
        if g in (0, 3):
            add(f"yf{g}", lambda c, sl=sl: act.at[c, 1, sl], lambda c, sl=sl: act.at[c, 3, sl], y_right)
        else:
            add(f"yf{g}", lambda c, sl=sl: act.at[c, 2, sl], lambda c, sl=sl: act.at[c, 3, sl], y_left)
    for i, peer in ((1, y_right), (2, y_left), (3, y_far)):
        add(f"gy{i}", lambda c: gact.at[c, 0, 0], lambda c, i=i: gact.at[c, 0, i], peer)
    for h in range(2):
        add(f"xop{h}", lambda c, h=h: part.at[c, h, xo, lo_half], lambda c, h=h: opp_in.at[c, h, 0], x_right)
        add(f"xom{h}", lambda c, h=h: part.at[c, h, xo, hi_half], lambda c, h=h: opp_in.at[c, h, 1], x_left)
        add(f"xdp{h}", lambda c, h=h: part.at[c, h, xr, hi_half], lambda c, h=h: sum_in.at[c, h, 0, hi_half], x_right)
        add(f"xdm{h}", lambda c, h=h: part.at[c, h, xl, lo_half], lambda c, h=h: sum_in.at[c, h, 1, lo_half], x_left)
        add(f"xsp{h}", lambda c, h=h: part.at[c, h, xr, lo_half], lambda c, h=h: sum_in.at[c, h, 0, lo_half], x_right)
        add(f"xsm{h}", lambda c, h=h: part.at[c, h, xl, hi_half], lambda c, h=h: sum_in.at[c, h, 1, hi_half], x_left)
        add(f"xap{h}", lambda c, h=h: share.at[c, h, x], lambda c, h=h: share.at[c, h, x], x_right,
            lambda c, h=h: share.at[c, h, xl])
        add(f"xam{h}", lambda c, h=h: share.at[c, h, x], lambda c, h=h: share.at[c, h, x], x_left,
            lambda c, h=h: share.at[c, h, xr])
        add(f"xfp{h}", lambda c, h=h: share.at[c, h, xl, lo_half], lambda c, h=h: share.at[c, h, xl, lo_half], x_right,
            lambda c, h=h: share.at[c, h, xo, lo_half])
        add(f"xfm{h}", lambda c, h=h: share.at[c, h, xr, hi_half], lambda c, h=h: share.at[c, h, xr, hi_half], x_left,
            lambda c, h=h: share.at[c, h, xo, hi_half])
    slots = ((7, 6, 4, 2), (7, 5, 3, 1))
    for j in range(2):
        pair = pl.ds(2 * j, 2)
        for way in range(2):
            for step in range(0 if j == way else 1, 4):
                add(f"r{j}{way}{step}", lambda c, s=slots[way][step], pair=pair: outs.at[c, s, pair],
                    lambda c, w=way, s=step, pair=pair: ring_in.at[c, w, s, pair], (z_right, z_left)[way])
    for i, (name, place, peer) in enumerate((("tp", 2, y_right), ("tm", 1, y_left), ("tf", 3, y_far))):
        add(name, lambda c, a=place: rows_out.at[c, a], lambda c, i=i: rows_in.at[c, i], peer)
    for g, (a, b) in enumerate(SUM_GROUPS):
        sl = pl.ds(a, b - a)
        for i, (place, peer) in enumerate(((1, y_left), (2, y_right), (3, y_far))):
            add(f"c{g}{i}", lambda c, a=place, sl=sl: gouts.at[c, a, sl], lambda c, i=i, sl=sl: col_in.at[c, i, sl], peer)
    for way in range(2):
        for step in range(1 - way, 4):
            add(f"q{way}{step}", lambda c, s=slots[way][step]: gouts.at[c, 0, s],
                lambda c, w=way, s=step: gring_in.at[c, w, s], (z_right, z_left)[way])
    assert len(copies) == send_sem.shape[1], len(copies)

    def describe(src, dst, c, index, peer):
        return pltpu.make_async_remote_copy(
            src_ref=src, dst_ref=dst, send_sem=send_sem.at[c, index], recv_sem=recv_sem.at[c, index],
            device_id=peer, device_id_type=MESH,
        )

    def start(c, *names):
        for name in names:
            index, src, dst, peer, land = copies[name]
            describe(src(c), dst(c), c, index, peer).start()

    def got(c, *names):
        for name in names:
            index, src, dst, peer, land = copies[name]
            describe(land(c), land(c), c, index, peer).wait_recv()

    def sent(c, *names):
        for name in names:
            index, src, dst, peer, land = copies[name]
            describe(src(c), dst(c), c, index, peer).wait_send()

    def mask_row(i):
        return (14 * z + i) // 4

    def load_gate_up(i):
        loads[i].wait()

        @pl.loop(0, tok_ref.shape[1] // EDGE)
        def _(f):
            at = pl.ds(pl.multiple_of(f * EDGE, EDGE), EDGE)
            turned[...] = window[i, at, :].T
            for g in range(14):
                rows = pl.ds(pl.multiple_of(lax.rem(z, 2) * 64 + g * GRAIN, GRAIN), GRAIN)
                keep = inner_ref[f, mask_row(g)].astype(F32)
                into = pl.ds(i * own + g % 7 * GRAIN, GRAIN)
                wgu[g // 7, into, at] = (turned[rows, :].astype(F32) * keep).astype(BF16)

    def load_down():
        loads[2].wait()
        loads[3].wait()

        @pl.loop(0, tok_ref.shape[1] // EDGE)
        def _(f):
            at = pl.ds(pl.multiple_of(f * EDGE, EDGE), EDGE)
            for g in range(14):
                rows = pl.ds(g % 7 * GRAIN, GRAIN)
                keep = outer_ref[f, mask_row(g)].astype(F32)
                wd[g // 7, rows, at] = (wd[g // 7, rows, at].astype(F32) * keep).astype(BF16)

    def gather(step, c):
        if step == 0:
            start(c, "gy1", "gy2", "gy3", "zp0", "zm0", "yp0", "ym0")
        elif step == 1:
            got(c, "gy1")
            start(c, "gp00", "gm00")
            got(c, "gy2", "gy3")
            start(c, "gp10", "gm10")
            got(c, "zp0", "zm0")
            start(c, "zp1", "zm1", "yp1", "ym1")
            got(c, "yp0", "ym0")
            start(c, "yf0")
        elif step == 2:
            got(c, "zp1", "zm1")
            start(c, "zp2", "zm2", "yp2", "ym2")
            for j in range(2):
                got(c, f"gp{j}0", f"gm{j}0")
                start(c, f"gp{j}1", f"gm{j}1")
        elif step == 3:
            got(c, "zp2", "zm2")
            start(c, "zp3")
            got(c, "yp1", "ym1")
            start(c, "yf1")
            for j in range(2):
                got(c, f"gp{j}1", f"gm{j}1")
                start(c, f"gp{j}2", f"gm{j}2")
        elif step == 4:
            got(c, "zp3")
            start(c, "yp3", "ym3")
            got(c, "yp2", "ym2")
            start(c, "yf2")
            got(c, "gp02", "gm02")
            start(c, "gp03")
            got(c, "gp12", "gm12")
            start(c, "gm13")
        elif step == 5:
            got(c, "yp3", "ym3")
            start(c, "yf3")
        else:
            for g in range(len(GROUPS)):
                got(c, f"yf{g}")
            got(c, "gp03", "gm13")

    def grad_rows(c, first_y, count, lanes):
        return jnp.concatenate(
            [gact[c, :, first_y + i, :, lanes].reshape(SLOTS * ROWS, -1) for i in range(count)], axis=0
        )

    def project(h, c):
        every = pl.ds(0, act.shape[-1])

        @pl.loop(0, 2)
        def _(p):
            gu = dot(wgu[h], act[c, pl.ds(2 * p, 2)].reshape(2 * SLOTS * ROWS, -1), (1, 1)).astype(BF16)
            part[c, h, 2 * p, pl.ds(0, unit)] = gu[:, :128]
            part[c, h, 2 * p + 1, pl.ds(0, unit)] = gu[:, 128:]
            hg = dot(wd[h], grad_rows(c, 2 * p, 2, every), (1, 1)).astype(BF16)
            part[c, h, 2 * p, pl.ds(unit, own)] = hg[:, :128]
            part[c, h, 2 * p + 1, pl.ds(unit, own)] = hg[:, 128:]

        start(c, f"xop{h}", f"xom{h}", f"xdp{h}", f"xdm{h}")

    tile = 112

    def middle_sums(h, c):
        got(c, f"xop{h}", f"xom{h}")

        @pl.loop(0, half // tile)
        def _(i):
            at = pl.ds(pl.multiple_of(i * tile, 16), tile)
            up = pl.ds(pl.multiple_of(half + i * tile, 16), tile)
            part[c, h, xr, at] = (part[c, h, xr, at].astype(F32) + opp_in[c, h, 0, at].astype(F32)).astype(BF16)
            part[c, h, xl, up] = (part[c, h, xl, up].astype(F32) + opp_in[c, h, 1, at].astype(F32)).astype(BF16)

        start(c, f"xsp{h}", f"xsm{h}")

    def gated(h, c):
        got(c, f"xdp{h}", f"xdm{h}", f"xsp{h}", f"xsm{h}")

        def total(at):
            return part[c, h, x, at].astype(F32) + sum_in[c, h, 0, at].astype(F32) + sum_in[c, h, 1, at].astype(F32)

        @pl.loop(0, own // GRAIN)
        def _(i):
            at = pl.ds(pl.multiple_of(i * GRAIN, GRAIN), GRAIN)
            at_up = pl.ds(pl.multiple_of(own + i * GRAIN, GRAIN), GRAIN)
            at_dn = pl.ds(pl.multiple_of(unit + i * GRAIN, GRAIN), GRAIN)
            gate, up, grad = total(at), total(at_up), total(at_dn)
            sig = 1.0 / (1.0 + jnp.exp(-gate))
            act_gate = gate * sig
            share[c, h, x, at_dn] = (act_gate * up).astype(BF16)
            share[c, h, x, at] = (grad * up * sig * (1.0 + gate * (1.0 - sig))).astype(BF16)
            share[c, h, x, at_up] = (grad * act_gate).astype(BF16)

        start(c, f"xap{h}", f"xam{h}")

    def forward_shares(h, c):
        got(c, f"xap{h}", f"xam{h}")
        start(c, f"xfp{h}", f"xfm{h}")

    def joined(c, h, rows, first_part, count):
        return jnp.concatenate([share[c, h, first_part + i, rows] for i in range(count)], axis=1)

    def both(c, rows, first_part, count):
        return jnp.concatenate([joined(c, h, rows, first_part, count) for h in range(2)], axis=0)

    def outputs(c):
        got(c, "xfp0", "xfm0", "xfp1", "xfm1")

        @pl.loop(0, 2)
        def _(p):
            left = both(c, pl.ds(unit, own), 2 * p, 2)
            done = dot(left, wd[...].reshape(unit, -1), (0, 0)).astype(BF16).reshape(2, SLOTS, ROWS, -1)
            outs[c, :, 2 * p] = done[0]
            outs[c, :, 2 * p + 1] = done[1]

        start(c, "r000", "r110", "r011", "r101")

        @pl.loop(0, 2)
        def _(p):
            left = both(c, pl.ds(0, unit), 2 * p, 2)
            done = dot(left, wgu[...].reshape(2 * unit, -1), (0, 0)).astype(BF16).reshape(2, SLOTS, ROWS, -1)
            gouts[c, 2 * p] = done[0]
            gouts[c, 2 * p + 1] = done[1]

        for g in range(len(SUM_GROUPS)):
            start(c, f"c{g}0", f"c{g}1", f"c{g}2")

    def ring(step, c):
        for j, way, n in ((0, 0, step), (1, 1, step), (0, 1, step + 1), (1, 0, step + 1)):
            if n > 3:
                continue
            got(c, f"r{j}{way}{n - 1}")
            slot = slots[way][n]
            for i in (2 * j, 2 * j + 1):
                outs[c, slot, i] = (outs[c, slot, i].astype(F32) + ring_in[c, way, n - 1, i].astype(F32)).astype(BF16)
            start(c, f"r{j}{way}{n}")

    def column(step, c):
        got(c, f"c{step}0", f"c{step}1", f"c{step}2")
        first, end = SUM_GROUPS[step]
        arriving = {}
        for way in range(2):
            if step > 1 - way:
                arriving[slots[way][step]] = way
        for slot in range(end - 1, first - 1, -1):
            total = gouts[c, 0, slot].astype(F32)
            for i in range(3):
                total = total + col_in[c, i, slot].astype(F32)
            if slot in arriving:
                way = arriving[slot]
                got(c, f"q{way}{step - 1}")
                total = total + gring_in[c, way, step - 1].astype(F32)
            gouts[c, 0, slot] = total.astype(BF16)
        for way in range(2):
            if step >= 1 - way:
                start(c, f"q{way}{step}")

    def finish_column(c):
        got(c, "q03", "q13")
        at = pl.ds(pl.multiple_of(c * ROWS, ROWS), ROWS)
        total = gouts[c, 0, 0].astype(F32) + gring_in[c, 0, 3].astype(F32) + gring_in[c, 1, 3].astype(F32)
        ig_ref[at, :] = total.astype(BF16)

    def own_sum(c, i):
        return outs[c, 0, i].astype(F32) + ring_in[c, 0, 3, i].astype(F32) + ring_in[c, 1, 3, i].astype(F32)

    def leave(c):
        got(c, "r003", "r013", "r103", "r113")
        for dest, name in ((3, "tf"), (2, "tp"), (1, "tm")):
            rows_out[c, dest] = own_sum(c, dest).astype(BF16)
            start(c, name)

    def finish_rows(c):
        at = pl.ds(pl.multiple_of(c * ROWS, ROWS), ROWS)
        got(c, "tp", "tm", "tf")
        total = own_sum(c, 0)
        for i in range(3):
            total = total + rows_in[c, i].astype(F32)
        lo_ref[at, :] = total.astype(BF16)

    width = 256

    def weight_grads(c):
        @pl.loop(0, acc.shape[2] // width)
        def _(n):
            lanes = pl.ds(pl.multiple_of(n * width, width), width)
            tokens = act[c, :, :, :, lanes].reshape(4 * SLOTS * ROWS, width)
            grads = grad_rows(c, 0, 4, lanes)
            for h in range(2):
                acc[h, pl.ds(0, unit), lanes] += dot(joined(c, h, pl.ds(0, unit), 0, 4), tokens, (1, 0))
                acc[h, pl.ds(unit, own), lanes] += dot(joined(c, h, pl.ds(unit, own), 0, 4), grads, (1, 0))

    def pair_copy():
        return pltpu.make_async_remote_copy(
            src_ref=pair_out, dst_ref=pair_in, send_sem=pair_send, recv_sem=pair_recv,
            device_id=sibling, device_id_type=MESH,
        )

    def pair_start():
        pair_out[...] = acc[1 - k].astype(BF16)
        pair_copy().start()

    def pair_finish():
        pair_copy().wait_recv()

        @pl.loop(0, tok_ref.shape[1] // EDGE)
        def _(f):
            at = pl.ds(pl.multiple_of(f * EDGE, EDGE), EDGE)
            for i, ref in enumerate((gate_ref, up_ref, down_ref)):
                pieces = []
                for g in range(7):
                    rows = pl.ds(i * own + g * GRAIN, GRAIN)
                    block = mask_row(7 * k + g)
                    keep = (inner_ref if i < 2 else outer_ref)[f, block].astype(F32)
                    pieces.append((acc[k, rows, at] + pair_in[rows, at].astype(F32)) * keep)
                ref[:, at] = jnp.concatenate(pieces, axis=0).astype(BF16)

    gather(0, 0)
    load_gate_up(0)
    gather(1, 0)
    load_gate_up(1)
    gather(2, 0)
    load_down()
    gather(3, 0)
    acc[...] = jnp.zeros_like(acc)

    @pl.loop(0, CHUNKS + 2)
    def _(s):
        ahead, now, behind = s, s - 1, s - 2

        def when_ahead(f, *a):
            pl.when(ahead < CHUNKS)(lambda: f(*a, ahead))

        def when_now(f, *a):
            pl.when((now >= 0) & (now < CHUNKS))(lambda: f(*a, now))

        def when_behind(f, *a):
            pl.when(behind >= 0)(lambda: f(*a, behind))

        def at_end(f):
            pl.when(s == CHUNKS + 1)(f)

        def when_next(f, *a):
            pl.when(s + 1 < CHUNKS)(lambda: f(*a, s + 1))

        when_now(middle_sums, 0)
        when_ahead(gather, 4)
        when_behind(ring, 1)
        when_now(middle_sums, 1)
        when_behind(column, 0)
        when_now(gated, 0)
        when_ahead(gather, 5)
        when_behind(ring, 2)
        when_now(gated, 1)
        when_behind(column, 1)
        when_next(gather, 0)
        when_ahead(gather, 6)
        when_behind(ring, 3)
        when_behind(weight_grads)
        at_end(pair_start)
        when_now(forward_shares, 0)
        when_next(gather, 1)
        when_behind(column, 2)
        when_ahead(project, 0)
        when_now(forward_shares, 1)
        when_ahead(project, 1)
        when_next(gather, 2)
        when_behind(leave)
        when_behind(column, 3)
        when_now(outputs)
        when_next(gather, 3)
        at_end(pair_finish)
        when_behind(finish_column)
        when_behind(finish_rows)
        pl.when(behind >= 0)(lambda: sent(behind, *copies))

    pair_copy().wait_send()


def on_device(tokens_in, out_grad, gate_weight, up_weight, down_weight, inner_mask, outer_mask):
    features, width = gate_weight.shape
    own = width // lax.axis_size("dp")
    rows = tokens_in.shape[0]
    full = 3 * own
    vmem = pl.BlockSpec(memory_space=pltpu.VMEM)
    smem = pl.BlockSpec(memory_space=pltpu.SMEM)
    anywhere = pl.BlockSpec(memory_space=pl.ANY)
    layer_out, input_grad, gate_grad, up_grad, down_grad = pl.pallas_call(
        layer_kernel,
        name="layer",
        out_shape=(
            jax.ShapeDtypeStruct((rows, features), BF16),
            jax.ShapeDtypeStruct((rows, features), BF16),
            jax.ShapeDtypeStruct((own, features), BF16),
            jax.ShapeDtypeStruct((own, features), BF16),
            jax.ShapeDtypeStruct((own, features), BF16),
        ),
        in_specs=[vmem, vmem, anywhere, anywhere, anywhere, smem, smem],
        out_specs=(vmem,) * 5,
        scratch_shapes=[
            pltpu.VMEM((CHUNKS, 4, SLOTS, ROWS, features), BF16),
            pltpu.VMEM((CHUNKS, SLOTS, 4, ROWS, features), BF16),
            pltpu.VMEM((CHUNKS, 2, 4, full, 128), BF16),
            pltpu.VMEM((CHUNKS, 2, 2, full // 2, 128), BF16),
            pltpu.VMEM((CHUNKS, 2, 2, full, 128), BF16),
            pltpu.VMEM((CHUNKS, 2, 4, full, 128), BF16),
            pltpu.VMEM((CHUNKS, SLOTS, 4, ROWS, features), BF16),
            pltpu.VMEM((CHUNKS, 4, SLOTS, ROWS, features), BF16),
            pltpu.VMEM((CHUNKS, 2, 4, 4, ROWS, features), BF16),
            pltpu.VMEM((CHUNKS, 2, 4, ROWS, features), BF16),
            pltpu.VMEM((CHUNKS, 3, SLOTS, ROWS, features), BF16),
            pltpu.VMEM((CHUNKS, 4, ROWS, features), BF16),
            pltpu.VMEM((CHUNKS, 3, ROWS, features), BF16),
            pltpu.VMEM((2, full, features), F32),
            pltpu.VMEM((full, features), BF16),
            pltpu.VMEM((full, features), BF16),
            pltpu.VMEM((2, 2 * own, features), BF16),
            pltpu.VMEM((2, own, features), BF16),
            pltpu.VMEM((2, features, WINDOW), BF16),
            pltpu.VMEM((WINDOW, EDGE), BF16),
            pltpu.SemaphoreType.DMA((CHUNKS, COPIES)),
            pltpu.SemaphoreType.DMA((CHUNKS, COPIES)),
            pltpu.SemaphoreType.DMA,
            pltpu.SemaphoreType.DMA,
            pltpu.SemaphoreType.DMA((4,)),
        ],
        compiler_params=pltpu.CompilerParams(
            collective_id=0, has_side_effects=True, vmem_limit_bytes=58 * 2**20
        ),
    )(tokens_in, out_grad, gate_weight, up_weight, down_weight, inner_mask, outer_mask.T)
    return (layer_out, input_grad, gate_grad.T, up_grad.T, down_grad)


def solution(mesh):
    placed = (
        P(("col", "dp"), "row"),
        P(("col", "dp"), "row"),
        P("row", "col"),
        P("row", "col"),
        P("col", "row"),
        P("row", "col"),
        P("col", "row"),
    )
    return jax.shard_map(
        on_device,
        mesh=mesh,
        in_specs=placed,
        out_specs=(
            P(("col", "dp"), "row"),
            P(("col", "dp"), "row"),
            P("row", ("col", "dp")),
            P("row", ("col", "dp")),
            P(("col", "dp"), "row"),
        ),
        check_vma=False,
    )
```

```python
import jax
import jax.numpy as jnp
from jax import lax
from jax.experimental import pallas as pl
from jax.experimental.pallas import tpu as pltpu
from jax.sharding import PartitionSpec as P

MESH = pl.DeviceIdType.MESH
F32 = jnp.float32
BF16 = jnp.bfloat16
CHUNKS = 3
ROWS = 16
SLOTS = 8
EDGE = 128
GRAIN = 32
WINDOW = 512
GROUPS = ((0, 1), (1, 3), (3, 5), (5, 8))
SUM_GROUPS = ((7, 8), (5, 7), (3, 5), (0, 3))
COPIES = 92


def dot(left, right, dims):
    return lax.dot_general(left, right, ((dims[:1], dims[1:]), ((), ())), preferred_element_type=F32)


def layer_kernel(
    tok_ref, grad_ref, gate_hbm, up_hbm, down_hbm, inner_ref, outer_ref,
    lo_ref, ig_ref, gate_ref, up_ref, down_ref,
    act, gact, part, opp_in, sum_in, share, outs, gouts, ring_in, gring_in, col_in, rows_out, rows_in, acc, pair_out, pair_in,
    wgu, wd, window, turned,
    send_sem, recv_sem, pair_send, pair_recv, load_sem,
):
    x = lax.axis_index("row")
    y = lax.axis_index("col")
    d = lax.axis_index("dp")
    z = d // 2
    k = lax.rem(d, 2)
    xr, xl, xo = lax.rem(x + 1, 4), lax.rem(x + 3, 4), lax.rem(x + 2, 4)
    x_right, x_left = (xr, y, d), (xl, y, d)
    y_right = (x, lax.rem(y + 1, 4), d)
    y_left = (x, lax.rem(y + 3, 4), d)
    y_far = (x, lax.rem(y + 2, 4), d)
    z_right = (x, y, lax.rem(z + 1, 8) * 2 + k)
    z_left = (x, y, lax.rem(z + 7, 8) * 2 + k)
    sibling = (x, y, z * 2 + 1 - k)
    own = wd.shape[1]
    unit = 2 * own
    full = part.shape[3]
    half = full // 2
    lo_half, hi_half = pl.ds(0, half), pl.ds(half, half)

    base = pl.multiple_of((7 * z) // 2 * EDGE, EDGE)
    loads = [
        pltpu.make_async_copy(gate_hbm.at[:, pl.ds(base, WINDOW)], window.at[0], load_sem.at[0]),
        pltpu.make_async_copy(up_hbm.at[:, pl.ds(base, WINDOW)], window.at[1], load_sem.at[1]),
    ]
    for h in range(2):
        rows = pl.ds(pl.multiple_of(z * unit + h * own, GRAIN), own)
        loads.append(pltpu.make_async_copy(down_hbm.at[rows, :], wd.at[h], load_sem.at[2 + h]))
    for load in loads:
        load.start()

    barrier = pltpu.get_barrier_semaphore()
    peers = (x_right, x_left, y_right, y_left, y_far, z_right, z_left, sibling)
    for peer in peers:
        pl.semaphore_signal(barrier, inc=1, device_id=peer, device_id_type=MESH)
    for c in range(CHUNKS):
        act[c, 0, 0] = tok_ref[pl.ds(c * ROWS, ROWS), :]
        gact[c, 0, 0] = grad_ref[pl.ds(c * ROWS, ROWS), :]
    pl.semaphore_wait(barrier, len(peers))

    copies = {}

    def add(name, src, dst, peer, land=None):
        copies[name] = (len(copies), src, dst, peer, dst if land is None else land)

    hops = (("p", (0, 1, 3, 5), (1, 3, 5, 7), z_right), ("m", (0, 2, 4, 6), (2, 4, 6, 7), z_left))
    for way, (letter, sources, targets, peer) in enumerate(hops):
        for step in range(4 if way == 0 else 3):
            add(f"z{letter}{step}", lambda c, a=sources[step]: act.at[c, 0, a], lambda c, a=targets[step]: act.at[c, 0, a], peer)
        for j in range(2):
            pair = pl.ds(2 * j, 2)
            for step in range(4 if way == j else 3):
                add(f"g{letter}{j}{step}", lambda c, a=sources[step], pair=pair: gact.at[c, a, pair],
                    lambda c, a=targets[step], pair=pair: gact.at[c, a, pair], peer)
    for g, (a, b) in enumerate(GROUPS):
        sl = pl.ds(a, b - a)
        add(f"yp{g}", lambda c, sl=sl: act.at[c, 0, sl], lambda c, sl=sl: act.at[c, 1, sl], y_right)
        add(f"ym{g}", lambda c, sl=sl: act.at[c, 0, sl], lambda c, sl=sl: act.at[c, 2, sl], y_left)
        if g in (0, 3):
            add(f"yf{g}", lambda c, sl=sl: act.at[c, 1, sl], lambda c, sl=sl: act.at[c, 3, sl], y_right)
        else:
            add(f"yf{g}", lambda c, sl=sl: act.at[c, 2, sl], lambda c, sl=sl: act.at[c, 3, sl], y_left)
    for i, peer in ((1, y_right), (2, y_left), (3, y_far)):
        add(f"gy{i}", lambda c: gact.at[c, 0, 0], lambda c, i=i: gact.at[c, 0, i], peer)
    for h in range(2):
        add(f"xop{h}", lambda c, h=h: part.at[c, h, xo, lo_half], lambda c, h=h: opp_in.at[c, h, 0], x_right)
        add(f"xom{h}", lambda c, h=h: part.at[c, h, xo, hi_half], lambda c, h=h: opp_in.at[c, h, 1], x_left)
        add(f"xdp{h}", lambda c, h=h: part.at[c, h, xr, hi_half], lambda c, h=h: sum_in.at[c, h, 0, hi_half], x_right)
        add(f"xdm{h}", lambda c, h=h: part.at[c, h, xl, lo_half], lambda c, h=h: sum_in.at[c, h, 1, lo_half], x_left)
        add(f"xsp{h}", lambda c, h=h: part.at[c, h, xr, lo_half], lambda c, h=h: sum_in.at[c, h, 0, lo_half], x_right)
        add(f"xsm{h}", lambda c, h=h: part.at[c, h, xl, hi_half], lambda c, h=h: sum_in.at[c, h, 1, hi_half], x_left)
        add(f"xap{h}", lambda c, h=h: share.at[c, h, x], lambda c, h=h: share.at[c, h, x], x_right,
            lambda c, h=h: share.at[c, h, xl])
        add(f"xam{h}", lambda c, h=h: share.at[c, h, x], lambda c, h=h: share.at[c, h, x], x_left,
            lambda c, h=h: share.at[c, h, xr])
        add(f"xfp{h}", lambda c, h=h: share.at[c, h, xl, lo_half], lambda c, h=h: share.at[c, h, xl, lo_half], x_right,
            lambda c, h=h: share.at[c, h, xo, lo_half])
        add(f"xfm{h}", lambda c, h=h: share.at[c, h, xr, hi_half], lambda c, h=h: share.at[c, h, xr, hi_half], x_left,
            lambda c, h=h: share.at[c, h, xo, hi_half])
    slots = ((7, 6, 4, 2), (7, 5, 3, 1))
    for j in range(2):
        pair = pl.ds(2 * j, 2)
        for way in range(2):
            for step in range(0 if j == way else 1, 4):
                add(f"r{j}{way}{step}", lambda c, s=slots[way][step], pair=pair: outs.at[c, s, pair],
                    lambda c, w=way, s=step, pair=pair: ring_in.at[c, w, s, pair], (z_right, z_left)[way])
    for i, (name, place, peer) in enumerate((("tp", 2, y_right), ("tm", 1, y_left), ("tf", 3, y_far))):
        add(name, lambda c, a=place: rows_out.at[c, a], lambda c, i=i: rows_in.at[c, i], peer)
    for g, (a, b) in enumerate(SUM_GROUPS):
        sl = pl.ds(a, b - a)
        for i, (place, peer) in enumerate(((1, y_left), (2, y_right), (3, y_far))):
            add(f"c{g}{i}", lambda c, a=place, sl=sl: gouts.at[c, a, sl], lambda c, i=i, sl=sl: col_in.at[c, i, sl], peer)
    for way in range(2):
        for step in range(1 - way, 4):
            add(f"q{way}{step}", lambda c, s=slots[way][step]: gouts.at[c, 0, s],
                lambda c, w=way, s=step: gring_in.at[c, w, s], (z_right, z_left)[way])
    assert len(copies) == send_sem.shape[1], len(copies)

    def describe(src, dst, c, index, peer):
        return pltpu.make_async_remote_copy(
            src_ref=src, dst_ref=dst, send_sem=send_sem.at[c, index], recv_sem=recv_sem.at[c, index],
            device_id=peer, device_id_type=MESH,
        )

    def start(c, *names):
        for name in names:
            index, src, dst, peer, land = copies[name]
            describe(src(c), dst(c), c, index, peer).start()

    def got(c, *names):
        for name in names:
            index, src, dst, peer, land = copies[name]
            describe(land(c), land(c), c, index, peer).wait_recv()

    def sent(c, *names):
        for name in names:
            index, src, dst, peer, land = copies[name]
            describe(src(c), dst(c), c, index, peer).wait_send()

    def mask_row(i):
        return (14 * z + i) // 4

    def load_gate_up(i):
        loads[i].wait()

        @pl.loop(0, tok_ref.shape[1] // EDGE)
        def _(f):
            at = pl.ds(pl.multiple_of(f * EDGE, EDGE), EDGE)
            turned[...] = window[i, at, :].T
            for g in range(14):
                rows = pl.ds(pl.multiple_of(lax.rem(z, 2) * 64 + g * GRAIN, GRAIN), GRAIN)
                keep = inner_ref[f, mask_row(g)].astype(F32)
                into = pl.ds(i * own + g % 7 * GRAIN, GRAIN)
                wgu[g // 7, into, at] = (turned[rows, :].astype(F32) * keep).astype(BF16)

    def load_down():
        loads[2].wait()
        loads[3].wait()

        @pl.loop(0, tok_ref.shape[1] // EDGE)
        def _(f):
            at = pl.ds(pl.multiple_of(f * EDGE, EDGE), EDGE)
            for g in range(14):
                rows = pl.ds(g % 7 * GRAIN, GRAIN)
                keep = outer_ref[f, mask_row(g)].astype(F32)
                wd[g // 7, rows, at] = (wd[g // 7, rows, at].astype(F32) * keep).astype(BF16)

    def gather(step, c):
        if step == 0:
            start(c, "gy1", "gy2", "gy3", "zp0", "zm0", "yp0", "ym0")
        elif step == 1:
            got(c, "gy1")
            start(c, "gp00", "gm00")
            got(c, "gy2", "gy3")
            start(c, "gp10", "gm10")
            got(c, "zp0", "zm0")
            start(c, "zp1", "zm1", "yp1", "ym1")
            got(c, "yp0", "ym0")
            start(c, "yf0")
        elif step == 2:
            got(c, "zp1", "zm1")
            start(c, "zp2", "zm2", "yp2", "ym2")
            for j in range(2):
                got(c, f"gp{j}0", f"gm{j}0")
                start(c, f"gp{j}1", f"gm{j}1")
        elif step == 3:
            got(c, "zp2", "zm2")
            start(c, "zp3")
            got(c, "yp1", "ym1")
            start(c, "yf1")
            for j in range(2):
                got(c, f"gp{j}1", f"gm{j}1")
                start(c, f"gp{j}2", f"gm{j}2")
        elif step == 4:
            got(c, "zp3")
            start(c, "yp3", "ym3")
            got(c, "yp2", "ym2")
            start(c, "yf2")
            got(c, "gp02", "gm02")
            start(c, "gp03")
            got(c, "gp12", "gm12")
            start(c, "gm13")
        elif step == 5:
            got(c, "yp3", "ym3")
            start(c, "yf3")
        else:
            for g in range(len(GROUPS)):
                got(c, f"yf{g}")
            got(c, "gp03", "gm13")

    def grad_rows(c, first_y, count, lanes):
        return jnp.concatenate(
            [gact[c, :, first_y + i, :, lanes].reshape(SLOTS * ROWS, -1) for i in range(count)], axis=0
        )

    def project(h, c):
        every = pl.ds(0, act.shape[-1])

        @pl.loop(0, 2)
        def _(p):
            gu = dot(wgu[h], act[c, pl.ds(2 * p, 2)].reshape(2 * SLOTS * ROWS, -1), (1, 1)).astype(BF16)
            part[c, h, 2 * p, pl.ds(0, unit)] = gu[:, :128]
            part[c, h, 2 * p + 1, pl.ds(0, unit)] = gu[:, 128:]
            hg = dot(wd[h], grad_rows(c, 2 * p, 2, every), (1, 1)).astype(BF16)
            part[c, h, 2 * p, pl.ds(unit, own)] = hg[:, :128]
            part[c, h, 2 * p + 1, pl.ds(unit, own)] = hg[:, 128:]

        start(c, f"xop{h}", f"xom{h}", f"xdp{h}", f"xdm{h}")

    tile = 112

    def middle_sums(h, c):
        got(c, f"xop{h}", f"xom{h}")

        @pl.loop(0, half // tile)
        def _(i):
            at = pl.ds(pl.multiple_of(i * tile, 16), tile)
            up = pl.ds(pl.multiple_of(half + i * tile, 16), tile)
            part[c, h, xr, at] = (part[c, h, xr, at].astype(F32) + opp_in[c, h, 0, at].astype(F32)).astype(BF16)
            part[c, h, xl, up] = (part[c, h, xl, up].astype(F32) + opp_in[c, h, 1, at].astype(F32)).astype(BF16)

        start(c, f"xsp{h}", f"xsm{h}")

    def gated(h, c):
        got(c, f"xdp{h}", f"xdm{h}", f"xsp{h}", f"xsm{h}")

        def total(at):
            return part[c, h, x, at].astype(F32) + sum_in[c, h, 0, at].astype(F32) + sum_in[c, h, 1, at].astype(F32)

        @pl.loop(0, own // GRAIN)
        def _(i):
            at = pl.ds(pl.multiple_of(i * GRAIN, GRAIN), GRAIN)
            at_up = pl.ds(pl.multiple_of(own + i * GRAIN, GRAIN), GRAIN)
            at_dn = pl.ds(pl.multiple_of(unit + i * GRAIN, GRAIN), GRAIN)
            gate, up, grad = total(at), total(at_up), total(at_dn)
            sig = 1.0 / (1.0 + jnp.exp(-gate))
            act_gate = gate * sig
            share[c, h, x, at_dn] = (act_gate * up).astype(BF16)
            share[c, h, x, at] = (grad * up * sig * (1.0 + gate * (1.0 - sig))).astype(BF16)
            share[c, h, x, at_up] = (grad * act_gate).astype(BF16)

        start(c, f"xap{h}", f"xam{h}")

    def forward_shares(h, c):
        got(c, f"xap{h}", f"xam{h}")
        start(c, f"xfp{h}", f"xfm{h}")

    def joined(c, h, rows, first_part, count):
        return jnp.concatenate([share[c, h, first_part + i, rows] for i in range(count)], axis=1)

    def both(c, rows, first_part, count):
        return jnp.concatenate([joined(c, h, rows, first_part, count) for h in range(2)], axis=0)

    def outputs(c):
        got(c, "xfp0", "xfm0", "xfp1", "xfm1")

        @pl.loop(0, 2)
        def _(p):
            left = both(c, pl.ds(unit, own), 2 * p, 2)
            done = dot(left, wd[...].reshape(unit, -1), (0, 0)).astype(BF16).reshape(2, SLOTS, ROWS, -1)
            outs[c, :, 2 * p] = done[0]
            outs[c, :, 2 * p + 1] = done[1]

        start(c, "r000", "r110", "r011", "r101")

        @pl.loop(0, 2)
        def _(p):
            left = both(c, pl.ds(0, unit), 2 * p, 2)
            done = dot(left, wgu[...].reshape(2 * unit, -1), (0, 0)).astype(BF16).reshape(2, SLOTS, ROWS, -1)
            gouts[c, 2 * p] = done[0]
            gouts[c, 2 * p + 1] = done[1]

        for g in range(len(SUM_GROUPS)):
            start(c, f"c{g}0", f"c{g}1", f"c{g}2")

    def ring(step, c):
        for j, way, n in ((0, 0, step), (1, 1, step), (0, 1, step + 1), (1, 0, step + 1)):
            if n > 3:
                continue
            got(c, f"r{j}{way}{n - 1}")
            slot = slots[way][n]
            for i in (2 * j, 2 * j + 1):
                outs[c, slot, i] = (outs[c, slot, i].astype(F32) + ring_in[c, way, n - 1, i].astype(F32)).astype(BF16)
            start(c, f"r{j}{way}{n}")

    def column(step, c):
        got(c, f"c{step}0", f"c{step}1", f"c{step}2")
        first, end = SUM_GROUPS[step]
        arriving = {}
        for way in range(2):
            if step > 1 - way:
                arriving[slots[way][step]] = way
        for slot in range(end - 1, first - 1, -1):
            total = gouts[c, 0, slot].astype(F32)
            for i in range(3):
                total = total + col_in[c, i, slot].astype(F32)
            if slot in arriving:
                way = arriving[slot]
                got(c, f"q{way}{step - 1}")
                total = total + gring_in[c, way, step - 1].astype(F32)
            gouts[c, 0, slot] = total.astype(BF16)
        for way in range(2):
            if step >= 1 - way:
                start(c, f"q{way}{step}")

    def finish_column(c):
        got(c, "q03", "q13")
        at = pl.ds(pl.multiple_of(c * ROWS, ROWS), ROWS)
        total = gouts[c, 0, 0].astype(F32) + gring_in[c, 0, 3].astype(F32) + gring_in[c, 1, 3].astype(F32)
        ig_ref[at, :] = total.astype(BF16)

    def own_sum(c, i):
        return outs[c, 0, i].astype(F32) + ring_in[c, 0, 3, i].astype(F32) + ring_in[c, 1, 3, i].astype(F32)

    def leave(c):
        got(c, "r003", "r013", "r103", "r113")
        for dest, name in ((3, "tf"), (2, "tp"), (1, "tm")):
            rows_out[c, dest] = own_sum(c, dest).astype(BF16)
            start(c, name)

    def finish_rows(c):
        at = pl.ds(pl.multiple_of(c * ROWS, ROWS), ROWS)
        got(c, "tp", "tm", "tf")
        total = own_sum(c, 0)
        for i in range(3):
            total = total + rows_in[c, i].astype(F32)
        lo_ref[at, :] = total.astype(BF16)

    width = 256

    def weight_grads(c):
        @pl.loop(0, acc.shape[2] // width)
        def _(n):
            lanes = pl.ds(pl.multiple_of(n * width, width), width)
            tokens = act[c, :, :, :, lanes].reshape(4 * SLOTS * ROWS, width)
            grads = grad_rows(c, 0, 4, lanes)
            for h in range(2):
                acc[h, pl.ds(0, unit), lanes] += dot(joined(c, h, pl.ds(0, unit), 0, 4), tokens, (1, 0))
                acc[h, pl.ds(unit, own), lanes] += dot(joined(c, h, pl.ds(unit, own), 0, 4), grads, (1, 0))

    def pair_copy():
        return pltpu.make_async_remote_copy(
            src_ref=pair_out, dst_ref=pair_in, send_sem=pair_send, recv_sem=pair_recv,
            device_id=sibling, device_id_type=MESH,
        )

    def pair_start():
        pair_out[...] = acc[1 - k].astype(BF16)
        pair_copy().start()

    def pair_finish():
        pair_copy().wait_recv()

        @pl.loop(0, tok_ref.shape[1] // EDGE)
        def _(f):
            at = pl.ds(pl.multiple_of(f * EDGE, EDGE), EDGE)
            for i, ref in enumerate((gate_ref, up_ref, down_ref)):
                pieces = []
                for g in range(7):
                    rows = pl.ds(i * own + g * GRAIN, GRAIN)
                    block = mask_row(7 * k + g)
                    keep = (inner_ref if i < 2 else outer_ref)[f, block].astype(F32)
                    pieces.append((acc[k, rows, at] + pair_in[rows, at].astype(F32)) * keep)
                ref[:, at] = jnp.concatenate(pieces, axis=0).astype(BF16)

    gather(0, 0)
    load_gate_up(0)
    gather(1, 0)
    load_gate_up(1)
    gather(2, 0)
    load_down()
    gather(3, 0)
    acc[...] = jnp.zeros_like(acc)

    @pl.loop(0, CHUNKS + 2)
    def _(s):
        ahead, now, behind = s, s - 1, s - 2

        def when_ahead(f, *a):
            pl.when(ahead < CHUNKS)(lambda: f(*a, ahead))

        def when_now(f, *a):
            pl.when((now >= 0) & (now < CHUNKS))(lambda: f(*a, now))

        def when_behind(f, *a):
            pl.when(behind >= 0)(lambda: f(*a, behind))

        def at_end(f):
            pl.when(s == CHUNKS + 1)(f)

        def when_next(f, *a):
            pl.when(s + 1 < CHUNKS)(lambda: f(*a, s + 1))

        when_now(middle_sums, 0)
        when_ahead(gather, 4)
        when_behind(ring, 1)
        when_now(middle_sums, 1)
        when_behind(column, 0)
        when_now(gated, 0)
        when_ahead(gather, 5)
        when_behind(ring, 2)
        when_now(gated, 1)
        when_behind(column, 1)
        when_next(gather, 0)
        when_ahead(gather, 6)
        when_behind(ring, 3)
        when_behind(weight_grads)
        at_end(pair_start)
        when_now(forward_shares, 0)
        when_next(gather, 1)
        when_behind(column, 2)
        when_now(forward_shares, 1)
        when_ahead(project, 0)
        when_ahead(project, 1)
        when_next(gather, 2)
        when_behind(leave)
        when_behind(column, 3)
        when_now(outputs)
        when_next(gather, 3)
        at_end(pair_finish)
        when_behind(finish_column)
        when_behind(finish_rows)
        pl.when(behind >= 0)(lambda: sent(behind, *copies))

    pair_copy().wait_send()


def on_device(tokens_in, out_grad, gate_weight, up_weight, down_weight, inner_mask, outer_mask):
    features, width = gate_weight.shape
    own = width // lax.axis_size("dp")
    rows = tokens_in.shape[0]
    full = 3 * own
    vmem = pl.BlockSpec(memory_space=pltpu.VMEM)
    smem = pl.BlockSpec(memory_space=pltpu.SMEM)
    anywhere = pl.BlockSpec(memory_space=pl.ANY)
    layer_out, input_grad, gate_grad, up_grad, down_grad = pl.pallas_call(
        layer_kernel,
        name="layer",
        out_shape=(
            jax.ShapeDtypeStruct((rows, features), BF16),
            jax.ShapeDtypeStruct((rows, features), BF16),
            jax.ShapeDtypeStruct((own, features), BF16),
            jax.ShapeDtypeStruct((own, features), BF16),
            jax.ShapeDtypeStruct((own, features), BF16),
        ),
        in_specs=[vmem, vmem, anywhere, anywhere, anywhere, smem, smem],
        out_specs=(vmem,) * 5,
        scratch_shapes=[
            pltpu.VMEM((CHUNKS, 4, SLOTS, ROWS, features), BF16),
            pltpu.VMEM((CHUNKS, SLOTS, 4, ROWS, features), BF16),
            pltpu.VMEM((CHUNKS, 2, 4, full, 128), BF16),
            pltpu.VMEM((CHUNKS, 2, 2, full // 2, 128), BF16),
            pltpu.VMEM((CHUNKS, 2, 2, full, 128), BF16),
            pltpu.VMEM((CHUNKS, 2, 4, full, 128), BF16),
            pltpu.VMEM((CHUNKS, SLOTS, 4, ROWS, features), BF16),
            pltpu.VMEM((CHUNKS, 4, SLOTS, ROWS, features), BF16),
            pltpu.VMEM((CHUNKS, 2, 4, 4, ROWS, features), BF16),
            pltpu.VMEM((CHUNKS, 2, 4, ROWS, features), BF16),
            pltpu.VMEM((CHUNKS, 3, SLOTS, ROWS, features), BF16),
            pltpu.VMEM((CHUNKS, 4, ROWS, features), BF16),
            pltpu.VMEM((CHUNKS, 3, ROWS, features), BF16),
            pltpu.VMEM((2, full, features), F32),
            pltpu.VMEM((full, features), BF16),
            pltpu.VMEM((full, features), BF16),
            pltpu.VMEM((2, 2 * own, features), BF16),
            pltpu.VMEM((2, own, features), BF16),
            pltpu.VMEM((2, features, WINDOW), BF16),
            pltpu.VMEM((WINDOW, EDGE), BF16),
            pltpu.SemaphoreType.DMA((CHUNKS, COPIES)),
            pltpu.SemaphoreType.DMA((CHUNKS, COPIES)),
            pltpu.SemaphoreType.DMA,
            pltpu.SemaphoreType.DMA,
            pltpu.SemaphoreType.DMA((4,)),
        ],
        compiler_params=pltpu.CompilerParams(
            collective_id=0, has_side_effects=True, vmem_limit_bytes=58 * 2**20
        ),
    )(tokens_in, out_grad, gate_weight, up_weight, down_weight, inner_mask, outer_mask.T)
    return (layer_out, input_grad, gate_grad.T, up_grad.T, down_grad)


def solution(mesh):
    placed = (
        P(("col", "dp"), "row"),
        P(("col", "dp"), "row"),
        P("row", "col"),
        P("row", "col"),
        P("col", "row"),
        P("row", "col"),
        P("col", "row"),
    )
    return jax.shard_map(
        on_device,
        mesh=mesh,
        in_specs=placed,
        out_specs=(
            P(("col", "dp"), "row"),
            P(("col", "dp"), "row"),
            P("row", ("col", "dp")),
            P("row", ("col", "dp")),
            P(("col", "dp"), "row"),
        ),
        check_vma=False,
    )
```
